256 devices in a mesh: frames: 32 (over z, x), heads: 8 (over y, core).
Axes of the slice: x: 4, y: 4, z: 8, core: 2. Of those that a mesh axis runs over, the one named last changes fastest.
Arguments:
- frames: bfloat16 [32768, 1024], P('frames', 'heads'), may hold values from -6 to 6
- latents: bfloat16 [512, 1024], replicated, may hold values from -6 to 6
- cross_query: bfloat16 [2, 1024, 1024], P(None, None, 'heads'), may hold values from -0.1875 to 0.1875
- cross_key: bfloat16 [2, 1024, 1024], P(None, None, 'heads'), may hold values from -0.1875 to 0.1875
- cross_value: bfloat16 [2, 1024, 1024], P(None, None, 'heads'), may hold values from -0.1875 to 0.1875
- cross_out: bfloat16 [2, 1024, 1024], P(None, 'heads'), may hold values from -0.1875 to 0.1875
- self_query: bfloat16 [2, 1024, 1024], P(None, None, 'heads'), may hold values from -0.1875 to 0.1875
- self_key: bfloat16 [2, 1024, 1024], P(None, None, 'heads'), may hold values from -0.1875 to 0.1875
- self_value: bfloat16 [2, 1024, 1024], P(None, None, 'heads'), may hold values from -0.1875 to 0.1875
- self_out: bfloat16 [2, 1024, 1024], P(None, 'heads'), may hold values from -0.1875 to 0.1875
- mlp_in: bfloat16 [2, 1024, 4096], P(None, None, 'heads'), may hold values from -0.1875 to 0.1875
- mlp_out: bfloat16 [2, 4096, 1024], P(None, 'heads'), may hold values from -0.09375 to 0.09375
Outputs:
- encoded: float32 [512, 1024], P('frames')
- midway: float32 [512, 1024], P(None, 'heads')
The draws below stay inside these ranges and needn't reach their ends.
All inputs are finite; a program needn't handle non-finite values.
Results may differ from the reference program's by a relative error of at most 0.007.
Values may be sent and summed in bfloat16 or wider, within the bound.
A program may use at most 64 MiB of HBM per device.

```python
import math
import jax
import jax.numpy as jnp
from jax import lax

D = 1024
HEADS = 16
HEAD_DIM = 64
LATENTS = 512
FF = 4096
PASSES = 2
FRAMES = 32768


def base_weight(key, seed_offset):
    random_part = jax.random.truncated_normal(jax.random.fold_in(key, seed_offset), -6.0, 6.0, (PASSES, D, D), jnp.float32)
    return random_part / math.sqrt(D)


def drawn_query(key, seed_offset):
    values = base_weight(key, seed_offset)
    return values.astype(jnp.bfloat16)


def drawn_key(key, seed_offset):
    values = base_weight(key, seed_offset)
    return values.astype(jnp.bfloat16)


def draw_cross_query(key, part):
    return drawn_query(key, 101)


def draw_cross_key(key, part):
    return drawn_key(key, 102)


def draw_self_query(key, part):
    return drawn_query(key, 103)


def draw_self_key(key, part):
    return drawn_key(key, 104)


def draw_frames(key, part):
    random_part = jax.random.truncated_normal(jax.random.fold_in(key, 31), -6.0, 6.0, (FRAMES, D), jnp.float32)
    return random_part.astype(jnp.bfloat16)


def draw_latents(key, part):
    random_part = jax.random.truncated_normal(jax.random.fold_in(key, 41), -6.0, 6.0, (LATENTS, D), jnp.float32)
    return random_part.astype(jnp.bfloat16)


def level_of(key, extent, cuts, least, top_value):
    level, own = 1.0, jax.random.fold_in(key, 6)
    for position, shards_of in cuts:
        steps = jnp.exp(jax.random.uniform(jax.random.fold_in(own, position), (shards_of,), jnp.float32, least / len(cuts), top_value / len(cuts)))
        level = level * jnp.repeat(steps, extent[position] // shards_of).reshape([-1 if axis == position else 1 for axis in range(len(extent))])
    return level


def centred(stream_key, shape, deviation, bound, shards=(), kind=jnp.bfloat16):
    entries = deviation * jax.random.normal(stream_key, shape, jnp.float32)
    if shards:
        entries = entries * level_of(stream_key, shape, shards, -0.22, 0.18)
    return jnp.clip(entries, -bound, bound).astype(kind)


def setup_inputs(seed: int = 0) -> dict:
    key_of = jax.random.split(jax.random.key(seed), 13)
    return {
        "frames": draw_frames(jax.random.fold_in(key_of[12], 71), 0),
        "latents": draw_latents(jax.random.fold_in(key_of[12], 71), 0),
        "cross_query": draw_cross_query(jax.random.fold_in(key_of[12], 71), 0),
        "cross_key": draw_cross_key(jax.random.fold_in(key_of[12], 71), 0),
        "cross_value": centred(key_of[4], (PASSES, D, D), D ** -0.5, 0.1875, ((2, 8),)),
        "cross_out": centred(key_of[5], (PASSES, D, D), D ** -0.5, 0.1875, ((1, 8),)),
        "self_query": draw_self_query(jax.random.fold_in(key_of[12], 71), 0),
        "self_key": draw_self_key(jax.random.fold_in(key_of[12], 71), 0),
        "self_value": centred(key_of[8], (PASSES, D, D), D ** -0.5, 0.1875, ((2, 8),)),
        "self_out": centred(key_of[9], (PASSES, D, D), D ** -0.5, 0.1875, ((1, 8),)),
        "mlp_in": centred(key_of[10], (PASSES, D, FF), D ** -0.5, 0.1875, ((2, 8),)),
        "mlp_out": centred(key_of[11], (PASSES, FF, D), FF ** -0.5, 0.09375, ((1, 8),)),
    }


epsilon = 1e-05

def layer_norm(vector):
    centre = vector - lax.optimization_barrier(jnp.mean(vector, axis=-1, keepdims=True))
    spread_sq = lax.optimization_barrier(jnp.mean(centre * centre, axis=-1, keepdims=True))
    return centre * lax.rsqrt(spread_sq + epsilon)

def project(left_side, weight):
    return jnp.dot(left_side, weight, preferred_element_type=jnp.float32)

def cross_context(queries, key_rows, value_rows):
    latent_count = queries.shape[0]
    frame_count = key_rows.shape[0]
    query_heads = queries.reshape(latent_count, HEADS, HEAD_DIM).transpose(1, 0, 2)
    key_heads = key_rows.reshape(frame_count, HEADS, HEAD_DIM).transpose(1, 0, 2)
    value_heads = value_rows.reshape(frame_count, HEADS, HEAD_DIM).transpose(1, 0, 2)

    def one_head(triple):
        query_one, key_one, value_one = triple
        scores = jnp.dot(query_one, key_one.T, preferred_element_type=jnp.float32)
        highest = lax.optimization_barrier(jnp.max(scores, axis=1, keepdims=True))
        exponent_terms = jnp.exp(scores - highest)
        totals = lax.optimization_barrier(jnp.sum(exponent_terms, axis=1, keepdims=True))
        weighted = jnp.dot(exponent_terms, value_one.astype(jnp.float32), precision=lax.Precision.HIGHEST)
        return (weighted / totals).astype(jnp.bfloat16)
    outcome = lax.map(one_head, (query_heads, key_heads, value_heads))
    return outcome.transpose(1, 0, 2).reshape(latent_count, HEADS * HEAD_DIM)

def self_context(queries, key_rows, value_rows):
    latent_count = queries.shape[0]
    query_heads = queries.reshape(latent_count, HEADS, HEAD_DIM).astype(jnp.float32)
    key_heads = key_rows.reshape(latent_count, HEADS, HEAD_DIM).astype(jnp.float32)
    value_heads = value_rows.reshape(latent_count, HEADS, HEAD_DIM).astype(jnp.float32)
    scores = jnp.einsum('ihd,khd->hik', query_heads, key_heads)
    weights = jax.nn.softmax(scores, axis=-1).astype(jnp.bfloat16)
    context = jnp.einsum('hik,khd->ihd', weights.astype(jnp.float32), value_heads)
    return context.reshape(latent_count, HEADS * HEAD_DIM).astype(jnp.bfloat16)

def reference(frames, latents, cross_query, cross_key, cross_value, cross_out, self_query, self_key, self_value, self_out, mlp_in, mlp_out):
    score_scale = 1.0 / HEAD_DIM ** 0.5
    normed = layer_norm(frames.astype(jnp.float32)).astype(jnp.bfloat16)
    latent_state = latents.astype(jnp.float32)
    midway = latent_state
    for pass_index in range(PASSES):
        cross_in = layer_norm(latent_state).astype(jnp.bfloat16)
        queries = (project(cross_in, cross_query[pass_index]) * score_scale).astype(jnp.bfloat16)
        key_rows = project(normed, cross_key[pass_index]).astype(jnp.bfloat16)
        value_rows = project(normed, cross_value[pass_index]).astype(jnp.bfloat16)
        context = cross_context(queries, key_rows, value_rows)
        latent_state = latent_state + project(context, cross_out[pass_index])
        self_in = layer_norm(latent_state).astype(jnp.bfloat16)
        self_q = (project(self_in, self_query[pass_index]) * score_scale).astype(jnp.bfloat16)
        self_k = project(self_in, self_key[pass_index]).astype(jnp.bfloat16)
        self_v = project(self_in, self_value[pass_index]).astype(jnp.bfloat16)
        context = self_context(self_q, self_k, self_v)
        latent_state = latent_state + project(context, self_out[pass_index])
        mlp_norm = layer_norm(latent_state).astype(jnp.bfloat16)
        hidden = jax.nn.gelu(project(mlp_norm, mlp_in[pass_index]), approximate=False).astype(jnp.bfloat16)
        latent_state = latent_state + project(hidden, mlp_out[pass_index])
        if pass_index == 0:
            midway = latent_state
    return (latent_state, midway)
```

```python
import functools

import jax
import jax.numpy as jnp
from jax import lax
from jax.experimental import pallas as pl
from jax.experimental.pallas import tpu as pltpu
from jax.sharding import PartitionSpec as P

EPSILON = 1e-05
HEAD_DIM = 64
MESH = pl.DeviceIdType.MESH
F32 = jnp.float32
BF16 = jnp.bfloat16
CHUNKS = 4
LANES = 128
ONES = 16
PART, STAT, CROSS, KEYS, SELF, MLP, QUERY, MID = range(8)


def layer_norm(v):
    centre = v - jnp.mean(v, axis=-1, keepdims=True)
    spread = jnp.mean(centre * centre, axis=-1, keepdims=True)
    return centre * lax.rsqrt(spread + EPSILON)


def project(a, b):
    return jnp.dot(a, b, preferred_element_type=F32)


def against(a, b):
    return lax.dot_general(a, b, (((1,), (1,)), ((), ())), preferred_element_type=F32)


def lane(shape):
    return lax.broadcasted_iota(jnp.int32, shape, len(shape) - 1)


def by_head(q):
    first = lane(q.shape) < HEAD_DIM
    zero = jnp.zeros_like(q)
    return jnp.concatenate([jnp.where(first, q, zero), jnp.where(first, zero, q)], axis=0)


def kernel(
    nf, nh,
    frames, latents, cq, ck, cv, co, sq, sk, sv, so, mi, mo,
    encoded, midway,
    x_s, lat_s, cq_s, ckv_s, co_s, sqkv_s, so_s, mi_s, mo_s,
    k_s, vt_s, qall_s, m_s, acc_s, o_s, st_s, po_s, ps_s, tr_s, kv_s, sum_s, row_s, mid_s,
    w_sem, own_sem, ring_recv, ring_send, recv_sem, send_sem,
):
    f, h = lax.axis_index("frames"), lax.axis_index("heads")
    latent_count, width = lat_s.shape
    frame_count = x_s.shape[0]
    rows_each = latent_count // nf
    chunk = frame_count // CHUNKS
    half = chunk // 2
    passes = cq_s.shape[0]

    sib = h + 1 - 2 * lax.rem(h, 2)
    right, left, opp = lax.rem(h + 2, nh), lax.rem(h + nh - 2, nh), lax.rem(h + 4, nh)

    def cols(who):
        return pl.ds(pl.multiple_of(who * LANES, LANES), LANES)

    own_rows = pl.ds(pl.multiple_of(f * rows_each, rows_each), rows_each)

    def local_copies():
        groups = [
            [(latents, lat_s)],
            [(cq, cq_s)],
            [(w.at[p], ckv_s.at[:, pl.ds((2 * p + i) * LANES, LANES)]) for p in range(passes) for i, w in enumerate((ck, cv))],
            [(co, co_s)],
            [(w, sqkv_s.at[:, :, pl.ds(i * LANES, LANES)]) for i, w in enumerate((sq, sk, sv))],
            [(so, so_s)],
            [(mi, mi_s)],
            [(mo, mo_s)],
        ]
        return groups

    for k in range(CHUNKS):
        r = pl.ds(k * chunk, chunk)
        pltpu.make_async_copy(frames.at[r, :], x_s.at[r, cols(h)], own_sem.at[k]).start()
    for i, group in enumerate(local_copies()):
        for src, dst in group:
            pltpu.make_async_copy(src, dst, w_sem.at[i]).start()

    def loaded(i, ref):
        pltpu.make_async_copy(ref, ref, w_sem.at[i]).wait()

    barrier = pltpu.get_barrier_semaphore()

    def greet_f(p, _):
        pl.semaphore_signal(barrier, inc=1, device_id=(lax.rem(f + p, nf), h), device_id_type=MESH)
        return 0

    def greet_h(p, _):
        pl.semaphore_signal(barrier, inc=1, device_id=(f, lax.rem(h + p, nh)), device_id_type=MESH)
        return 0

    lax.fori_loop(1, nh, greet_h, 0)
    lax.fori_loop(1, nf, greet_f, 0)
    pl.semaphore_wait(barrier, nf + nh - 2)

    L, R, OA, OB, S_OWN, S_L, S_R, S_OA, S_OB = range(9)

    def ring(kind, k, src, dst, to):
        return pltpu.make_async_remote_copy(
            src, dst, ring_send, ring_recv.at[kind, k], device_id=(f, to), device_id_type=MESH
        )

    def block(k, who, part=None):
        start, size = (k * chunk, chunk) if part is None else (k * chunk + part * half, half)
        return x_s.at[pl.ds(pl.multiple_of(start, half), size), cols(who)]

    def arrived(kind, k, ref):
        ring(kind, k, ref, ref, sib).wait_recv()

    def send_own(k, _):
        src = frames.at[pl.ds(pl.multiple_of(k * chunk, chunk), chunk), :]
        ring(L, k, src, block(k, h), right).start()
        ring(R, k, src, block(k, h), left).start()
        ring(S_OWN, k, src, block(k, h), sib).start()
        return 0

    lax.fori_loop(0, CHUNKS, send_own, 0)

    def set_queries(p, q):
        qall_s[p] = q

    loaded(0, lat_s)
    loaded(1, cq_s)
    state = lat_s[...].astype(F32)
    q0 = (project(layer_norm(state).astype(BF16), cq_s[0]) * 0.125).astype(BF16)
    set_queries(0, q0)
    rows = lat_s[own_rows, :].astype(F32)
    for p in range(passes):
        vt_s[p, pl.ds(LANES, ONES), :] = jnp.ones((ONES, frame_count), BF16)
    loaded(2, ckv_s)

    def keys_values(k):
        r = pl.ds(pl.multiple_of(k * chunk, chunk), chunk)
        normed = layer_norm(x_s[r, :].astype(F32)).astype(BF16)
        both = project(normed, ckv_s[...])
        for p in range(passes):
            k_s[p, r, :] = both[:, 2 * p * LANES:(2 * p + 1) * LANES].astype(BF16)
            value = both[:, (2 * p + 1) * LANES:(2 * p + 2) * LANES]
            vt_s[p, pl.ds(0, LANES), r] = value.T.astype(BF16)

    def attend_start():
        m_s[...] = jnp.full_like(m_s, -jnp.inf)
        acc_s[...] = jnp.zeros_like(acc_s)

    def attend(p, k):
        r = pl.ds(pl.multiple_of(k * chunk, chunk), chunk)
        scores = against(k_s[p, r, :], by_head(qall_s[p]))
        before = m_s[...]
        highest = jnp.maximum(before, jnp.max(scores, axis=0, keepdims=True))
        terms = jnp.exp(scores - highest).astype(BF16)
        acc_s[...] = acc_s[...] * jnp.exp(before - highest) + project(vt_s[p, :, r], terms)
        m_s[...] = highest

    def exchange_f(kind, p, pairs):
        def send(d, _):
            t = lax.rem(f + d, nf)
            for i, (src_of, dst, _all) in enumerate(pairs):
                pltpu.make_async_remote_copy(
                    src_of(t), dst, send_sem.at[p, kind + i], recv_sem.at[p, kind + i],
                    device_id=(t, h), device_id_type=MESH,
                ).start()
            return 0
        lax.fori_loop(1, nf, send, 0)

    def landed(kind, p, ref):
        pltpu.make_async_remote_copy(
            ref, ref, send_sem.at[p, kind], recv_sem.at[p, kind], device_id=(f, sib), device_id_type=MESH
        ).wait_recv()

    def sent(kind, p, ref):
        pltpu.make_async_remote_copy(
            ref, ref, send_sem.at[p, kind], recv_sem.at[p, kind], device_id=(f, sib), device_id_type=MESH
        ).wait_send()

    def attend_end(p):
        total = acc_s[pl.ds(LANES, 1), :]
        value = acc_s[pl.ds(0, LANES), :] / total
        both = jnp.concatenate(
            [value[:HEAD_DIM, :latent_count], value[HEAD_DIM:, latent_count:]], axis=0
        )
        o_s[p] = both.T.astype(BF16)
        level = m_s[...] + jnp.log(total)
        for t in range(latent_count // LANES):
            for i in range(2):
                at = i * latent_count + t * LANES
                st_s[p, t, pl.ds(i, 1), :] = level[:, at:at + LANES]

        def rows_of(t):
            return pl.ds(pl.multiple_of(t * rows_each, rows_each), rows_each)

        per_tile = LANES // rows_each
        exchange_f(PART, p, [
            (lambda t: o_s.at[p, rows_of(t), :], po_s.at[p, f], None),
            (lambda t: st_s.at[p, t // per_tile], ps_s.at[p, f], None),
        ])
        po_s[p, f] = o_s[p, own_rows, :]
        ps_s[p, f] = st_s[p, f // per_tile]
        landed(STAT, p, ps_s.at[p, pl.ds(0, nf - 1)])
        levels = jnp.concatenate([ps_s[p, :, 0, :], ps_s[p, :, 1, :]], axis=0)
        tr_s[...] = levels.T
        mine = tr_s[pl.ds(pl.multiple_of(lax.rem(f, per_tile) * rows_each, rows_each), rows_each), :]
        weights = []
        for i in range(2):
            level = mine[:, i * nf:(i + 1) * nf]
            e = jnp.exp(level - jnp.max(level, axis=1, keepdims=True))
            weights.append(e / jnp.sum(e, axis=1, keepdims=True))
        landed(PART, p, po_s.at[p, pl.ds(0, nf - 1)])
        first = lane((rows_each, LANES)) < HEAD_DIM
        context = jnp.zeros((rows_each, LANES), F32)
        for s in range(nf):
            w = jnp.where(first, weights[0][:, s:s + 1], weights[1][:, s:s + 1])
            context += w * po_s[p, s].astype(F32)
        return context.astype(BF16)

    def head_total(kind, slot, p, part):
        sum_s[p, slot, h] = part.astype(BF16)

        def send(d, _):
            t = lax.rem(h + d, nh)
            pltpu.make_async_remote_copy(
                sum_s.at[p, slot, h], sum_s.at[p, slot, h], send_sem.at[p, kind], recv_sem.at[p, kind],
                device_id=(f, t), device_id_type=MESH,
            ).start()
            return 0

        lax.fori_loop(1, nh, send, 0)
        landed(kind, p, sum_s.at[p, slot, pl.ds(0, nh - 1)])
        out = sum_s[p, slot, 0].astype(F32)
        for i in range(1, nh):
            out += sum_s[p, slot, i].astype(F32)
        return out

    attend_start()

    def step(j, _):
        @pl.when(j < CHUNKS)
        def _():
            arrived(L, j, block(j, left))
            arrived(R, j, block(j, right))
            ring(OA, j, block(j, left, 0), block(j, left, 0), right).start()
            ring(OB, j, block(j, right, 1), block(j, right, 1), left).start()
            ring(S_L, j, block(j, left), block(j, left), sib).start()
            ring(S_R, j, block(j, right), block(j, right), sib).start()

        @pl.when(jnp.logical_and(j >= 1, j <= CHUNKS))
        def _():
            k = j - 1
            arrived(OA, k, block(k, opp, 0))
            arrived(OB, k, block(k, opp, 1))
            ring(S_OA, k, block(k, opp, 0), block(k, opp, 0), sib).start()
            ring(S_OB, k, block(k, opp, 1), block(k, opp, 1), sib).start()

        @pl.when(j >= 2)
        def _():
            k = j - 2
            r = pl.ds(pl.multiple_of(k * chunk, chunk), chunk)
            pltpu.make_async_copy(frames.at[r, :], x_s.at[r, cols(h)], own_sem.at[k]).wait()
            for kind in (S_OWN, S_L, S_R):
                arrived(kind, k, block(k, sib))
            for part, kind in enumerate((S_OA, S_OB)):
                arrived(kind, k, block(k, sib, part))
            keys_values(k)
            attend(0, k)

        return 0

    lax.fori_loop(0, CHUNKS + 2, step, 0)

    for p in range(passes):
        if p > 0:
            attend_start()

            def again(k, _):
                attend(p, k)
                return 0

            lax.fori_loop(0, CHUNKS, again, 0)
        context = attend_end(p)
        if p == 0:
            loaded(3, co_s)
        rows = rows + head_total(CROSS, 0, p, project(context, co_s[p]))

        if p == 0:
            loaded(4, sqkv_s)
        self_qkv = project(layer_norm(rows).astype(BF16), sqkv_s[p])
        kv_s[p, own_rows, :] = self_qkv[:, LANES:].astype(BF16)
        exchange_f(KEYS, p, [(lambda t: kv_s.at[p, own_rows, :], kv_s.at[p, own_rows, :], None)])
        q = by_head((self_qkv[:, :LANES] * 0.125).astype(BF16))
        landed(KEYS, p, kv_s.at[p, pl.ds(0, latent_count - rows_each)])
        scores = against(q, kv_s[p, :, pl.ds(0, LANES)])
        e = jnp.exp(scores - jnp.max(scores, axis=1, keepdims=True))
        weight = (e / jnp.sum(e, axis=1, keepdims=True)).astype(BF16)
        both = project(weight, kv_s[p, :, pl.ds(LANES, LANES)])
        first = lane((rows_each, LANES)) < HEAD_DIM
        context = jnp.where(first, both[:rows_each], both[rows_each:]).astype(BF16)
        if p == 0:
            loaded(5, so_s)
        rows = rows + head_total(SELF, 1, p, project(context, so_s[p]))

        if p == 0:
            loaded(6, mi_s)
        u = project(layer_norm(rows).astype(BF16), mi_s[p])
        hidden = (0.5 * u * (1.0 + lax.erf(u * 0.7071067811865476))).astype(BF16)
        if p == 0:
            loaded(7, mo_s)
        rows = rows + head_total(MLP, 2, p, project(hidden, mo_s[p]))

        if p + 1 < passes:
            q = (project(layer_norm(rows).astype(BF16), cq_s[p + 1]) * 0.125).astype(BF16)
            qall_s[p + 1, own_rows, :] = q
            here = qall_s.at[p + 1, own_rows, :]
            exchange_f(QUERY, p, [(lambda t: here, here, None)])
        if p == 0:
            row_s[...] = rows
            source, there = row_s.at[:, cols(h)], mid_s.at[own_rows, :]
            exchange_f(MID, p, [(lambda t: source, there, None)])
            mid_s[own_rows, :] = row_s[:, cols(h)]
        if p + 1 < passes:
            landed(QUERY, p, qall_s.at[p + 1, pl.ds(0, latent_count - rows_each)])

    encoded[...] = rows
    landed(MID, 0, mid_s.at[pl.ds(0, latent_count - rows_each)])
    midway[...] = mid_s[...]

    ring(0, 0, x_s.at[:, pl.ds(0, 7 * LANES)], x_s.at[:, pl.ds(0, 7 * LANES)], sib).wait_send()
    for p in range(passes):
        sent(PART, p, po_s.at[p, pl.ds(0, nf - 1)])
        sent(STAT, p, ps_s.at[p, pl.ds(0, nf - 1)])
        sent(KEYS, p, kv_s.at[p, pl.ds(0, latent_count - rows_each)])
        for slot, kind in enumerate((CROSS, SELF, MLP)):
            sent(kind, p, sum_s.at[p, slot, pl.ds(0, nh - 1)])
        if p + 1 < passes:
            sent(QUERY, p, qall_s.at[p + 1, pl.ds(0, latent_count - rows_each)])
    sent(MID, 0, mid_s.at[pl.ds(0, latent_count - rows_each)])


def local(nf, nh, *args):
    frames, latents, cq, mi = args[0], args[1], args[2], args[10]
    frame_count = frames.shape[0]
    latent_count, width = latents.shape
    passes, hidden = cq.shape[0], mi.shape[2]
    rows_each = latent_count // nf
    vm = pltpu.VMEM
    scratch = [
        vm((frame_count, width), BF16),
        vm((latent_count, width), BF16),
        vm((passes, width, LANES), BF16),
        vm((width, 2 * passes * LANES), BF16),
        vm((passes, LANES, width), BF16),
        vm((passes, width, 3 * LANES), BF16),
        vm((passes, LANES, width), BF16),
        vm((passes, width, hidden), BF16),
        vm((passes, hidden, width), BF16),
        vm((passes, frame_count, LANES), BF16),
        vm((passes, LANES + ONES, frame_count), BF16),
        vm((passes, latent_count, LANES), BF16),
        vm((1, 2 * latent_count), F32),
        vm((LANES + ONES, 2 * latent_count), F32),
        vm((passes, latent_count, LANES), BF16),
        vm((passes, latent_count // LANES, 2, LANES), F32),
        vm((passes, nf, rows_each, LANES), BF16),
        vm((passes, nf, 2, LANES), F32),
        vm((LANES, 2 * nf), F32),
        vm((passes, latent_count, 2 * LANES), BF16),
        vm((passes, 3, nh, rows_each, width), BF16),
        vm((rows_each, width), F32),
        vm((latent_count, LANES), F32),
        pltpu.SemaphoreType.DMA((8,)),
        pltpu.SemaphoreType.DMA((CHUNKS,)),
        pltpu.SemaphoreType.DMA((9, CHUNKS)),
        pltpu.SemaphoreType.DMA(()),
        pltpu.SemaphoreType.DMA((passes, 8)),
        pltpu.SemaphoreType.DMA((passes, 8)),
    ]
    return pl.pallas_call(
        functools.partial(kernel, nf, nh),
        out_shape=(
            jax.ShapeDtypeStruct((rows_each, width), F32),
            jax.ShapeDtypeStruct((latent_count, LANES), F32),
        ),
        in_specs=[pl.BlockSpec(memory_space=pl.ANY)] * len(args),
        out_specs=(pl.BlockSpec(memory_space=vm), pl.BlockSpec(memory_space=vm)),
        scratch_shapes=scratch,
        compiler_params=pltpu.CompilerParams(
            collective_id=0, has_side_effects=True, vmem_limit_bytes=56 * 1024 * 1024
        ),
    )(*args)


def solution(mesh):
    nf, nh = mesh.shape["frames"], mesh.shape["heads"]
    by_column, by_row = P(None, None, "heads"), P(None, "heads", None)
    placed = (
        P("frames", "heads"), P(),
        by_column, by_column, by_column, by_row,
        by_column, by_column, by_column, by_row,
        by_column, by_row,
    )
    return jax.shard_map(
        functools.partial(local, nf, nh),
        mesh=mesh,
        in_specs=placed,
        out_specs=(P("frames", None), P(None, "heads")),
        check_vma=False,
    )
```

```python
import functools

import jax
import jax.numpy as jnp
from jax import lax
from jax.experimental import pallas as pl
from jax.experimental.pallas import tpu as pltpu
from jax.sharding import PartitionSpec as P

EPSILON = 1e-05
HEAD_DIM = 64
MESH = pl.DeviceIdType.MESH
F32 = jnp.float32
BF16 = jnp.bfloat16
CHUNKS = 4
LANES = 128
ONES = 16
PART, STAT, CROSS, KEYS, VALUES, SELF, MLP, QUERY, MID = range(9)


def layer_norm(v):
    centre = v - jnp.mean(v, axis=-1, keepdims=True)
    spread = jnp.mean(centre * centre, axis=-1, keepdims=True)
    return centre * lax.rsqrt(spread + EPSILON)


def project(a, b):
    return jnp.dot(a, b, preferred_element_type=F32)


def against(a, b):
    return lax.dot_general(a, b, (((1,), (1,)), ((), ())), preferred_element_type=F32)


def lane(shape):
    return lax.broadcasted_iota(jnp.int32, shape, len(shape) - 1)


def by_head(q):
    first = lane(q.shape) < HEAD_DIM
    zero = jnp.zeros_like(q)
    return jnp.concatenate([jnp.where(first, q, zero), jnp.where(first, zero, q)], axis=0)


def farthest_first(nz, nx):
    steps = [(dz, dx) for dz in range(nz) for dx in range(nx) if dz or dx]
    return sorted(steps, key=lambda s: -(min(s[0], nz - s[0]) + min(s[1], nx - s[1])))


def kernel(
    nf, nh,
    frames, latents, cq, ck, cv, co, sq, sk, sv, so, mi, mo,
    encoded, midway,
    x_s, lat_s, cq_s, ckv_s, co_s, sqkv_s, so_s, mi_s, mo_s,
    k_s, vt_s, qall_s, qh_s, m_s, acc_s, o_s, st_s, po_s, ps_s, tr_s, sk_s, sv_s, sum_s, row_s, mid_s,
    w_sem, own_sem, ring_recv, ring_send, recv_sem, send_sem,
):
    f, h = lax.axis_index("frames"), lax.axis_index("heads")
    latent_count, width = lat_s.shape
    frame_count = x_s.shape[0]
    rows_each = latent_count // nf
    chunk = frame_count // CHUNKS
    half = chunk // 2
    passes = cq_s.shape[0]

    sib = h + 1 - 2 * lax.rem(h, 2)
    right, left, opp = lax.rem(h + 2, nh), lax.rem(h + nh - 2, nh), lax.rem(h + 4, nh)

    def cols(who):
        return pl.ds(pl.multiple_of(who * LANES, LANES), LANES)

    own_rows = pl.ds(pl.multiple_of(f * rows_each, rows_each), rows_each)

    def local_copies():
        groups = [
            [(latents, lat_s)],
            [(cq, cq_s)],
            [(w.at[p], ckv_s.at[:, pl.ds((2 * p + i) * LANES, LANES)]) for p in range(passes) for i, w in enumerate((ck, cv))],
            [(co, co_s)],
            [(w, sqkv_s.at[:, :, pl.ds(i * LANES, LANES)]) for i, w in enumerate((sq, sk, sv))],
            [(so, so_s)],
            [(mi, mi_s)],
            [(mo, mo_s)],
        ]
        return groups

    for k in range(CHUNKS):
        r = pl.ds(k * chunk, chunk)
        pltpu.make_async_copy(frames.at[r, :], x_s.at[r, cols(h)], own_sem.at[k]).start()
    for i, group in enumerate(local_copies()):
        for src, dst in group:
            pltpu.make_async_copy(src, dst, w_sem.at[i]).start()

    def loaded(i, ref):
        pltpu.make_async_copy(ref, ref, w_sem.at[i]).wait()

    barrier = pltpu.get_barrier_semaphore()

    nx = 4
    nz = nf // nx
    z, x = f // nx, lax.rem(f, nx)

    def frames_peers():
        for dz, dx in farthest_first(nz, nx):
            yield lax.rem(z + dz, nz) * nx + lax.rem(x + dx, nx)

    def greet_h(p, _):
        pl.semaphore_signal(barrier, inc=1, device_id=(f, lax.rem(h + p, nh)), device_id_type=MESH)
        return 0

    for t in frames_peers():
        pl.semaphore_signal(barrier, inc=1, device_id=(t, h), device_id_type=MESH)
    lax.fori_loop(1, nh, greet_h, 0)
    pl.semaphore_wait(barrier, nf + nh - 2)

    L, R, OA, OB, S_OWN, S_L, S_R, S_OA, S_OB = range(9)

    def ring(kind, k, src, dst, to):
        return pltpu.make_async_remote_copy(
            src, dst, ring_send, ring_recv.at[kind, k], device_id=(f, to), device_id_type=MESH
        )

    def block(k, who, part=None):
        start, size = (k * chunk, chunk) if part is None else (k * chunk + part * half, half)
        return x_s.at[pl.ds(pl.multiple_of(start, half), size), cols(who)]

    def arrived(kind, k, ref):
        ring(kind, k, ref, ref, sib).wait_recv()

    def send_own(k, _):
        src = frames.at[pl.ds(pl.multiple_of(k * chunk, chunk), chunk), :]
        ring(L, k, src, block(k, h), right).start()
        ring(R, k, src, block(k, h), left).start()
        ring(S_OWN, k, src, block(k, h), sib).start()
        return 0

    lax.fori_loop(0, CHUNKS, send_own, 0)

    loaded(0, lat_s)
    loaded(1, cq_s)
    state = lat_s[...].astype(F32)
    q0 = (project(layer_norm(state).astype(BF16), cq_s[0]) * 0.125).astype(BF16)
    qh_s[...] = by_head(q0)
    rows = lat_s[own_rows, :].astype(F32)
    for p in range(passes):
        vt_s[p, pl.ds(LANES, ONES), :] = jnp.ones((ONES, frame_count), BF16)
    loaded(2, ckv_s)

    def keys_values(k):
        r = pl.ds(pl.multiple_of(k * chunk, chunk), chunk)
        normed = layer_norm(x_s[r, :].astype(F32)).astype(BF16)
        both = project(normed, ckv_s[...])
        for p in range(passes):
            k_s[p, r, :] = both[:, 2 * p * LANES:(2 * p + 1) * LANES].astype(BF16)
            value = both[:, (2 * p + 1) * LANES:(2 * p + 2) * LANES]
            vt_s[p, pl.ds(0, LANES), r] = value.T.astype(BF16)

    def attend_start():
        m_s[...] = jnp.full_like(m_s, -jnp.inf)
        acc_s[...] = jnp.zeros_like(acc_s)

    def attend(p, k):
        r = pl.ds(pl.multiple_of(k * chunk, chunk), chunk)
        scores = against(k_s[p, r, :], qh_s[...])
        before = m_s[...]
        highest = jnp.maximum(before, jnp.max(scores, axis=0, keepdims=True))
        terms = jnp.exp(scores - highest).astype(BF16)
        acc_s[...] = acc_s[...] * jnp.exp(before - highest) + project(vt_s[p, :, r], terms)
        m_s[...] = highest

    outstanding = []

    def exchange_f(kind, p, source, there, everything):
        for t in frames_peers():
            pltpu.make_async_remote_copy(
                source(t), there, send_sem.at[p, kind], recv_sem.at[p, kind],
                device_id=(t, h), device_id_type=MESH,
            ).start()
        outstanding.append(lambda: sent(kind, p, everything))

    def landed(kind, p, ref):
        pltpu.make_async_remote_copy(
            ref, ref, send_sem.at[p, kind], recv_sem.at[p, kind], device_id=(f, sib), device_id_type=MESH
        ).wait_recv()

    def sent(kind, p, ref):
        pltpu.make_async_remote_copy(
            ref, ref, send_sem.at[p, kind], recv_sem.at[p, kind], device_id=(f, sib), device_id_type=MESH
        ).wait_send()

    def attend_end(p):
        total = acc_s[pl.ds(LANES, 1), :]
        value = acc_s[pl.ds(0, LANES), :] / total
        both = jnp.concatenate(
            [value[:HEAD_DIM, :latent_count], value[HEAD_DIM:, latent_count:]], axis=0
        )
        o_s[p] = both.T.astype(BF16)
        level = m_s[...] + jnp.log(total)
        for t in range(latent_count // LANES):
            for i in range(2):
                at = i * latent_count + t * LANES
                st_s[p, t, pl.ds(i, 1), :] = level[:, at:at + LANES]

        def rows_of(t):
            return pl.ds(pl.multiple_of(t * rows_each, rows_each), rows_each)

        per_tile = LANES // rows_each
        stats, parts = ps_s.at[p, pl.ds(0, nf - 1)], po_s.at[p, pl.ds(0, nf - 1)]
        exchange_f(STAT, p, lambda t: st_s.at[p, t // per_tile], ps_s.at[p, f], stats)
        exchange_f(PART, p, lambda t: o_s.at[p, rows_of(t), :], po_s.at[p, f], parts)
        po_s[p, f] = o_s[p, own_rows, :]
        ps_s[p, f] = st_s[p, f // per_tile]
        landed(STAT, p, stats)
        levels = jnp.concatenate([ps_s[p, :, 0, :], ps_s[p, :, 1, :]], axis=0)
        tr_s[...] = levels.T
        mine = tr_s[pl.ds(pl.multiple_of(lax.rem(f, per_tile) * rows_each, rows_each), rows_each), :]
        weights = []
        for i in range(2):
            level = mine[:, i * nf:(i + 1) * nf]
            e = jnp.exp(level - jnp.max(level, axis=1, keepdims=True))
            weights.append(e / jnp.sum(e, axis=1, keepdims=True))
        landed(PART, p, parts)
        first = lane((rows_each, LANES)) < HEAD_DIM
        context = jnp.zeros((rows_each, LANES), F32)
        for s in range(nf):
            w = jnp.where(first, weights[0][:, s:s + 1], weights[1][:, s:s + 1])
            context += w * po_s[p, s].astype(F32)
        return context.astype(BF16)

    def head_total(kind, slot, p, part):
        sum_s[p, slot, h] = part.astype(BF16)

        def send(d, _):
            t = lax.rem(h + d, nh)
            pltpu.make_async_remote_copy(
                sum_s.at[p, slot, h], sum_s.at[p, slot, h], send_sem.at[p, kind], recv_sem.at[p, kind],
                device_id=(f, t), device_id_type=MESH,
            ).start()
            return 0

        lax.fori_loop(1, nh, send, 0)
        outstanding.append(lambda: sent(kind, p, sum_s.at[p, slot, pl.ds(0, nh - 1)]))
        landed(kind, p, sum_s.at[p, slot, pl.ds(0, nh - 1)])
        out = sum_s[p, slot, 0].astype(F32)
        for i in range(1, nh):
            out += sum_s[p, slot, i].astype(F32)
        return out

    attend_start()

    def step(j, _):
        @pl.when(j < CHUNKS)
        def _():
            arrived(L, j, block(j, left))
            arrived(R, j, block(j, right))
            ring(OA, j, block(j, left, 0), block(j, left, 0), right).start()
            ring(OB, j, block(j, right, 1), block(j, right, 1), left).start()
            ring(S_L, j, block(j, left), block(j, left), sib).start()
            ring(S_R, j, block(j, right), block(j, right), sib).start()

        @pl.when(jnp.logical_and(j >= 1, j <= CHUNKS))
        def _():
            k = j - 1
            arrived(OA, k, block(k, opp, 0))
            arrived(OB, k, block(k, opp, 1))
            ring(S_OA, k, block(k, opp, 0), block(k, opp, 0), sib).start()
            ring(S_OB, k, block(k, opp, 1), block(k, opp, 1), sib).start()

        @pl.when(j >= 2)
        def _():
            k = j - 2
            r = pl.ds(pl.multiple_of(k * chunk, chunk), chunk)
            pltpu.make_async_copy(frames.at[r, :], x_s.at[r, cols(h)], own_sem.at[k]).wait()
            for kind in (S_OWN, S_L, S_R):
                arrived(kind, k, block(k, sib))
            for part, kind in enumerate((S_OA, S_OB)):
                arrived(kind, k, block(k, sib, part))
            keys_values(k)
            attend(0, k)

        return 0

    lax.fori_loop(0, CHUNKS + 2, step, 0)

    for p in range(passes):
        if p > 0:
            attend_start()
            qh_s[...] = by_head(qall_s[p])

            def again(k, _):
                attend(p, k)
                return 0

            lax.fori_loop(0, CHUNKS, again, 0)
        context = attend_end(p)
        if p == 0:
            loaded(3, co_s)
        rows = rows + head_total(CROSS, 0, p, project(context, co_s[p]))

        if p == 0:
            loaded(4, sqkv_s)
        self_qkv = project(layer_norm(rows).astype(BF16), sqkv_s[p])
        others = pl.ds(0, latent_count - rows_each)
        for i, (kind, ref) in enumerate(((KEYS, sk_s), (VALUES, sv_s))):
            ref[p, own_rows, :] = self_qkv[:, (i + 1) * LANES:(i + 2) * LANES].astype(BF16)
            here = ref.at[p, own_rows, :]
            exchange_f(kind, p, lambda t: here, here, ref.at[p, others, :])
        q = by_head((self_qkv[:, :LANES] * 0.125).astype(BF16))
        landed(KEYS, p, sk_s.at[p, others, :])
        scores = against(q, sk_s[p])
        e = jnp.exp(scores - jnp.max(scores, axis=1, keepdims=True))
        weight = (e / jnp.sum(e, axis=1, keepdims=True)).astype(BF16)
        landed(VALUES, p, sv_s.at[p, others, :])
        both = project(weight, sv_s[p])
        first = lane((rows_each, LANES)) < HEAD_DIM
        context = jnp.where(first, both[:rows_each], both[rows_each:]).astype(BF16)
        if p == 0:
            loaded(5, so_s)
        rows = rows + head_total(SELF, 1, p, project(context, so_s[p]))

        if p == 0:
            loaded(6, mi_s)
        u = project(layer_norm(rows).astype(BF16), mi_s[p])
        hidden = (0.5 * u * (1.0 + lax.erf(u * 0.7071067811865476))).astype(BF16)
        if p == 0:
            loaded(7, mo_s)
        rows = rows + head_total(MLP, 2, p, project(hidden, mo_s[p]))

        if p + 1 < passes:
            q = (project(layer_norm(rows).astype(BF16), cq_s[p + 1]) * 0.125).astype(BF16)
            qall_s[p + 1, own_rows, :] = q
            here = qall_s.at[p + 1, own_rows, :]
            exchange_f(QUERY, p, lambda t: here, here, qall_s.at[p + 1, others, :])
        if p == 0:
            row_s[...] = rows
            source, there = row_s.at[:, cols(h)], mid_s.at[own_rows, :]
            exchange_f(MID, p, lambda t: source, there, mid_s.at[others, :])
            mid_s[own_rows, :] = row_s[:, cols(h)]
        if p + 1 < passes:
            landed(QUERY, p, qall_s.at[p + 1, others, :])

    encoded[...] = rows
    landed(MID, 0, mid_s.at[pl.ds(0, latent_count - rows_each)])
    midway[...] = mid_s[...]

    ring(0, 0, x_s.at[:, pl.ds(0, 7 * LANES)], x_s.at[:, pl.ds(0, 7 * LANES)], sib).wait_send()
    for wait in outstanding:
        wait()


def local(nf, nh, *args):
    frames, latents, cq, mi = args[0], args[1], args[2], args[10]
    frame_count = frames.shape[0]
    latent_count, width = latents.shape
    passes, hidden = cq.shape[0], mi.shape[2]
    rows_each = latent_count // nf
    vm = pltpu.VMEM
    scratch = [
        vm((frame_count, width), BF16),
        vm((latent_count, width), BF16),
        vm((passes, width, LANES), BF16),
        vm((width, 2 * passes * LANES), BF16),
        vm((passes, LANES, width), BF16),
        vm((passes, width, 3 * LANES), BF16),
        vm((passes, LANES, width), BF16),
        vm((passes, width, hidden), BF16),
        vm((passes, hidden, width), BF16),
        vm((passes, frame_count, LANES), BF16),
        vm((passes, LANES + ONES, frame_count), BF16),
        vm((passes, latent_count, LANES), BF16),
        vm((2 * latent_count, LANES), BF16),
        vm((1, 2 * latent_count), F32),
        vm((LANES + ONES, 2 * latent_count), F32),
        vm((passes, latent_count, LANES), BF16),
        vm((passes, latent_count // LANES, 2, LANES), F32),
        vm((passes, nf, rows_each, LANES), BF16),
        vm((passes, nf, 2, LANES), F32),
        vm((LANES, 2 * nf), F32),
        vm((passes, latent_count, LANES), BF16),
        vm((passes, latent_count, LANES), BF16),
        vm((passes, 3, nh, rows_each, width), BF16),
        vm((rows_each, width), F32),
        vm((latent_count, LANES), F32),
        pltpu.SemaphoreType.DMA((8,)),
        pltpu.SemaphoreType.DMA((CHUNKS,)),
        pltpu.SemaphoreType.DMA((9, CHUNKS)),
        pltpu.SemaphoreType.DMA(()),
        pltpu.SemaphoreType.DMA((passes, 9)),
        pltpu.SemaphoreType.DMA((passes, 9)),
    ]
    return pl.pallas_call(
        functools.partial(kernel, nf, nh),
        out_shape=(
            jax.ShapeDtypeStruct((rows_each, width), F32),
            jax.ShapeDtypeStruct((latent_count, LANES), F32),
        ),
        in_specs=[pl.BlockSpec(memory_space=pl.ANY)] * len(args),
        out_specs=(pl.BlockSpec(memory_space=vm), pl.BlockSpec(memory_space=vm)),
        scratch_shapes=scratch,
        compiler_params=pltpu.CompilerParams(
            collective_id=0, has_side_effects=True, vmem_limit_bytes=56 * 1024 * 1024
        ),
    )(*args)


def solution(mesh):
    nf, nh = mesh.shape["frames"], mesh.shape["heads"]
    by_column, by_row = P(None, None, "heads"), P(None, "heads", None)
    placed = (
        P("frames", "heads"), P(),
        by_column, by_column, by_column, by_row,
        by_column, by_column, by_column, by_row,
        by_column, by_row,
    )
    return jax.shard_map(
        functools.partial(local, nf, nh),
        mesh=mesh,
        in_specs=placed,
        out_specs=(P("frames", None), P(None, "heads")),
        check_vma=False,
    )
```

```python
import functools

import jax
import jax.numpy as jnp
from jax import lax
from jax.experimental import pallas as pl
from jax.experimental.pallas import tpu as pltpu
from jax.sharding import PartitionSpec as P

EPSILON = 1e-05
HEAD_DIM = 64
MESH = pl.DeviceIdType.MESH
F32 = jnp.float32
BF16 = jnp.bfloat16
CHUNKS = 4
LANES = 128
ONES = 16
PART, STAT, KEYS, VALUES, QUERY, MID, CROSS, SELF, MLP = range(9)
PAIRS = 3


def layer_norm(v):
    centre = v - jnp.mean(v, axis=-1, keepdims=True)
    spread = jnp.mean(centre * centre, axis=-1, keepdims=True)
    return centre * lax.rsqrt(spread + EPSILON)


def project(a, b):
    return jnp.dot(a, b, preferred_element_type=F32)


def against(a, b):
    return lax.dot_general(a, b, (((1,), (1,)), ((), ())), preferred_element_type=F32)


def lane(shape):
    return lax.broadcasted_iota(jnp.int32, shape, len(shape) - 1)


def by_head(q):
    first = lane(q.shape) < HEAD_DIM
    zero = jnp.zeros_like(q)
    return jnp.concatenate([jnp.where(first, q, zero), jnp.where(first, zero, q)], axis=0)


def farthest_first(nz, nx):
    steps = [(dz, dx) for dz in range(nz) for dx in range(nx) if dz or dx]
    return sorted(steps, key=lambda s: -(min(s[0], nz - s[0]) + min(s[1], nx - s[1])))


def kernel(
    nf, nh,
    frames, latents, cq, ck, cv, co, sq, sk, sv, so, mi, mo,
    encoded, midway,
    x_s, lat_s, cq_s, ckv_s, co_s, sqkv_s, so_s, mi_s, mo_s,
    k_s, vt_s, qall_s, qh_s, m_s, acc_s, o_s, st_s, po_s, ps_s, tr_s, sk_s, sv_s, give_s, take_s, sum_s, row_s, mid_s,
    w_sem, own_sem, ring_recv, ring_send, recv_sem, send_sem,
):
    f, h = lax.axis_index("frames"), lax.axis_index("heads")
    latent_count, width = lat_s.shape
    frame_count = x_s.shape[0]
    rows_each = latent_count // nf
    chunk = frame_count // CHUNKS
    half = width // 2
    passes = cq_s.shape[0]

    sib = h + 1 - 2 * lax.rem(h, 2)
    right, left, opp = lax.rem(h + 2, nh), lax.rem(h + nh - 2, nh), lax.rem(h + 4, nh)

    def cols(who):
        return pl.ds(pl.multiple_of(who * LANES, LANES), LANES)

    own_rows = pl.ds(pl.multiple_of(f * rows_each, rows_each), rows_each)

    def local_copies():
        groups = [
            [(latents, lat_s)],
            [(cq, cq_s)],
            [(w.at[p], ckv_s.at[:, pl.ds((2 * p + i) * LANES, LANES)]) for p in range(passes) for i, w in enumerate((ck, cv))],
            [(co, co_s)],
            [(w, sqkv_s.at[:, :, pl.ds(i * LANES, LANES)]) for i, w in enumerate((sq, sk, sv))],
            [(so, so_s)],
            [(mi, mi_s)],
            [(mo, mo_s)],
        ]
        return groups

    for k in range(CHUNKS):
        r = pl.ds(k * chunk, chunk)
        pltpu.make_async_copy(frames.at[r, :], x_s.at[r, cols(h)], own_sem.at[k]).start()
    for i, group in enumerate(local_copies()):
        for src, dst in group:
            pltpu.make_async_copy(src, dst, w_sem.at[i]).start()

    def loaded(i, ref):
        pltpu.make_async_copy(ref, ref, w_sem.at[i]).wait()

    barrier = pltpu.get_barrier_semaphore()

    nx = 4
    nz = nf // nx
    z, x = f // nx, lax.rem(f, nx)

    def frames_peers():
        for dz, dx in farthest_first(nz, nx):
            yield lax.rem(z + dz, nz) * nx + lax.rem(x + dx, nx)

    def greet_h(p, _):
        pl.semaphore_signal(barrier, inc=1, device_id=(f, lax.rem(h + p, nh)), device_id_type=MESH)
        return 0

    for t in frames_peers():
        pl.semaphore_signal(barrier, inc=1, device_id=(t, h), device_id_type=MESH)
    lax.fori_loop(1, nh, greet_h, 0)
    pl.semaphore_wait(barrier, nf + nh - 2)

    L, R, O, S_OWN, S_L, S_R, S_O = range(7)

    def ring(kind, k, src, dst, to):
        return pltpu.make_async_remote_copy(
            src, dst, ring_send, ring_recv.at[kind, k], device_id=(f, to), device_id_type=MESH
        )

    def block(k, who):
        return x_s.at[pl.ds(k * chunk, chunk), cols(who)]

    def arrived(kind, k, who):
        ring(kind, k, block(k, who), block(k, who), sib).wait_recv()

    def pass_on(kind, k, who, to):
        ring(kind, k, block(k, who), block(k, who), to).start()

    evens, odds = range(0, CHUNKS, 2), range(1, CHUNKS, 2)
    for a, b in zip((*evens, *odds), (*odds, *evens)):
        for kind, k, to in ((L, a, right), (R, b, left)):
            ring(kind, k, frames.at[pl.ds(k * chunk, chunk), :], block(k, h), to).start()
    for k in range(CHUNKS):
        ring(S_OWN, k, frames.at[pl.ds(k * chunk, chunk), :], block(k, h), sib).start()

    loaded(0, lat_s)
    loaded(1, cq_s)
    state = lat_s[...].astype(F32)
    q0 = (project(layer_norm(state).astype(BF16), cq_s[0]) * 0.125).astype(BF16)
    qh_s[...] = by_head(q0)
    rows = lat_s[own_rows, :].astype(F32)
    for p in range(passes):
        vt_s[p, pl.ds(LANES, ONES), :] = jnp.ones((ONES, frame_count), BF16)
    loaded(2, ckv_s)

    def keys_values(k):
        r = pl.ds(k * chunk, chunk)
        normed = layer_norm(x_s[r, :].astype(F32)).astype(BF16)
        both = project(normed, ckv_s[...])
        for p in range(passes):
            k_s[p, r, :] = both[:, 2 * p * LANES:(2 * p + 1) * LANES].astype(BF16)
            value = both[:, (2 * p + 1) * LANES:(2 * p + 2) * LANES]
            vt_s[p, pl.ds(0, LANES), r] = value.T.astype(BF16)

    def attend_start():
        m_s[...] = jnp.full_like(m_s, -jnp.inf)
        acc_s[...] = jnp.zeros_like(acc_s)

    def attend(p, k):
        r = pl.ds(pl.multiple_of(k * chunk, chunk), chunk)
        scores = against(k_s[p, r, :], qh_s[...])
        before = m_s[...]
        highest = jnp.maximum(before, jnp.max(scores, axis=0, keepdims=True))
        terms = jnp.exp(scores - highest).astype(BF16)
        acc_s[...] = acc_s[...] * jnp.exp(before - highest) + project(vt_s[p, :, r], terms)
        m_s[...] = highest

    outstanding = []

    def exchange_f(kind, p, source, there, everything):
        for t in frames_peers():
            pltpu.make_async_remote_copy(
                source(t), there, send_sem.at[p, kind], recv_sem.at[p, kind],
                device_id=(t, h), device_id_type=MESH,
            ).start()
        outstanding.append(lambda: sent(kind, p, everything))

    def landed(kind, p, ref):
        pltpu.make_async_remote_copy(
            ref, ref, send_sem.at[p, kind], recv_sem.at[p, kind], device_id=(f, sib), device_id_type=MESH
        ).wait_recv()

    def sent(kind, p, ref):
        pltpu.make_async_remote_copy(
            ref, ref, send_sem.at[p, kind], recv_sem.at[p, kind], device_id=(f, sib), device_id_type=MESH
        ).wait_send()

    def attend_end(p):
        total = acc_s[pl.ds(LANES, 1), :]
        value = acc_s[pl.ds(0, LANES), :] / total
        both = jnp.concatenate(
            [value[:HEAD_DIM, :latent_count], value[HEAD_DIM:, latent_count:]], axis=0
        )
        o_s[p] = both.T.astype(BF16)
        level = m_s[...] + jnp.log(total)
        for t in range(latent_count // LANES):
            for i in range(2):
                at = i * latent_count + t * LANES
                st_s[p, t, pl.ds(i, 1), :] = level[:, at:at + LANES]

        def rows_of(t):
            return pl.ds(pl.multiple_of(t * rows_each, rows_each), rows_each)

        per_tile = LANES // rows_each
        stats, parts = ps_s.at[p, pl.ds(0, nf - 1)], po_s.at[p, pl.ds(0, nf - 1)]
        exchange_f(STAT, p, lambda t: st_s.at[p, t // per_tile], ps_s.at[p, f], stats)
        exchange_f(PART, p, lambda t: o_s.at[p, rows_of(t), :], po_s.at[p, f], parts)
        po_s[p, f] = o_s[p, own_rows, :]
        ps_s[p, f] = st_s[p, f // per_tile]
        landed(STAT, p, stats)
        levels = jnp.concatenate([ps_s[p, :, 0, :], ps_s[p, :, 1, :]], axis=0)
        tr_s[...] = levels.T
        mine = tr_s[pl.ds(pl.multiple_of(lax.rem(f, per_tile) * rows_each, rows_each), rows_each), :]
        weights = []
        for i in range(2):
            level = mine[:, i * nf:(i + 1) * nf]
            e = jnp.exp(level - jnp.max(level, axis=1, keepdims=True))
            weights.append(e / jnp.sum(e, axis=1, keepdims=True))
        landed(PART, p, parts)
        first = lane((rows_each, LANES)) < HEAD_DIM
        context = jnp.zeros((rows_each, LANES), F32)
        for s in range(nf):
            w = jnp.where(first, weights[0][:, s:s + 1], weights[1][:, s:s + 1])
            context += w * po_s[p, s].astype(F32)
        return context.astype(BF16)

    core = lax.rem(h, 2)

    def half_of(c):
        return pl.ds(pl.multiple_of(c * half, half), half)

    def head_total(kind, slot, p, left_side, weight):
        give_s[p, slot] = project(left_side, weight[p, :, half_of(1 - core)]).astype(BF16)
        pair = pltpu.make_async_remote_copy(
            give_s.at[p, slot], take_s.at[p, slot], send_sem.at[p, kind + PAIRS], recv_sem.at[p, kind + PAIRS],
            device_id=(f, sib), device_id_type=MESH,
        )
        pair.start()
        mine = project(left_side, weight[p, :, half_of(core)])
        pair.wait()
        sum_s[p, slot, h] = (mine + take_s[p, slot].astype(F32)).astype(BF16)
        for d in (4, 5, 3, 2, 6, 7, 1):
            pltpu.make_async_remote_copy(
                sum_s.at[p, slot, h], sum_s.at[p, slot, h], send_sem.at[p, kind], recv_sem.at[p, kind],
                device_id=(f, lax.rem(h + d, nh)), device_id_type=MESH,
            ).start()
        outstanding.append(lambda: sent(kind, p, sum_s.at[p, slot, pl.ds(0, nh - 1)]))
        landed(kind, p, sum_s.at[p, slot, pl.ds(0, nh - 1)])
        halves = []
        for c in range(2):
            out = sum_s[p, slot, c].astype(F32)
            for i in range(c + 2, nh, 2):
                out += sum_s[p, slot, i].astype(F32)
            halves.append(out)
        return jnp.concatenate(halves, axis=1)

    attend_start()

    for k in range(CHUNKS):
        kind, onward, who, to = (L, S_L, left, right) if k % 2 == 0 else (R, S_R, right, left)
        arrived(kind, k, who)
        pass_on(O, k, who, to)
        pass_on(onward, k, who, sib)
    for k in (*odds, *evens):
        kind, onward, who = (R, S_R, right) if k % 2 == 0 else (L, S_L, left)
        arrived(kind, k, who)
        pass_on(onward, k, who, sib)
    for j in range(CHUNKS + 1):
        if j < CHUNKS:
            arrived(O, j, opp)
            pass_on(S_O, j, opp, sib)
        if j > 0:
            k = j - 1
            r = pl.ds(k * chunk, chunk)
            pltpu.make_async_copy(frames.at[r, :], x_s.at[r, cols(h)], own_sem.at[k]).wait()
            for kind in (S_OWN, S_L, S_R, S_O):
                arrived(kind, k, sib)
            keys_values(k)
            attend(0, k)

    for p in range(passes):
        if p > 0:
            attend_start()
            qh_s[...] = by_head(qall_s[p])

            def again(k, _):
                attend(p, k)
                return 0

            lax.fori_loop(0, CHUNKS, again, 0)
        context = attend_end(p)
        if p == 0:
            loaded(3, co_s)
        rows = rows + head_total(CROSS, 0, p, context, co_s)

        if p == 0:
            loaded(4, sqkv_s)
        self_in = layer_norm(rows).astype(BF16)
        others = pl.ds(0, latent_count - rows_each)
        for i, (kind, ref) in enumerate(((KEYS, sk_s), (VALUES, sv_s))):
            ref[p, own_rows, :] = project(self_in, sqkv_s[p, :, pl.ds((i + 1) * LANES, LANES)]).astype(BF16)
            here = ref.at[p, own_rows, :]
            exchange_f(kind, p, lambda t: here, here, ref.at[p, others, :])
        q = by_head((project(self_in, sqkv_s[p, :, pl.ds(0, LANES)]) * 0.125).astype(BF16))
        landed(KEYS, p, sk_s.at[p, others, :])
        scores = against(q, sk_s[p])
        e = jnp.exp(scores - jnp.max(scores, axis=1, keepdims=True))
        weight = (e / jnp.sum(e, axis=1, keepdims=True)).astype(BF16)
        landed(VALUES, p, sv_s.at[p, others, :])
        both = project(weight, sv_s[p])
        first = lane((rows_each, LANES)) < HEAD_DIM
        context = jnp.where(first, both[:rows_each], both[rows_each:]).astype(BF16)
        if p == 0:
            loaded(5, so_s)
        rows = rows + head_total(SELF, 1, p, context, so_s)

        if p == 0:
            loaded(6, mi_s)
        u = project(layer_norm(rows).astype(BF16), mi_s[p])
        hidden = (0.5 * u * (1.0 + lax.erf(u * 0.7071067811865476))).astype(BF16)
        if p == 0:
            loaded(7, mo_s)
        rows = rows + head_total(MLP, 2, p, hidden, mo_s)

        if p + 1 < passes:
            q = (project(layer_norm(rows).astype(BF16), cq_s[p + 1]) * 0.125).astype(BF16)
            qall_s[p + 1, own_rows, :] = q
            here = qall_s.at[p + 1, own_rows, :]
            exchange_f(QUERY, p, lambda t: here, here, qall_s.at[p + 1, others, :])
        if p == 0:
            row_s[...] = rows
            source, there = row_s.at[:, cols(h)], mid_s.at[own_rows, :]
            exchange_f(MID, p, lambda t: source, there, mid_s.at[others, :])
            mid_s[own_rows, :] = row_s[:, cols(h)]
        if p + 1 < passes:
            landed(QUERY, p, qall_s.at[p + 1, others, :])

    encoded[...] = rows
    landed(MID, 0, mid_s.at[pl.ds(0, latent_count - rows_each)])
    midway[...] = mid_s[...]

    ring(0, 0, x_s.at[:, pl.ds(0, 7 * LANES)], x_s.at[:, pl.ds(0, 7 * LANES)], sib).wait_send()
    for wait in outstanding:
        wait()


def local(nf, nh, *args):
    frames, latents, cq, mi = args[0], args[1], args[2], args[10]
    frame_count = frames.shape[0]
    latent_count, width = latents.shape
    passes, hidden = cq.shape[0], mi.shape[2]
    rows_each = latent_count // nf
    vm = pltpu.VMEM
    scratch = [
        vm((frame_count, width), BF16),
        vm((latent_count, width), BF16),
        vm((passes, width, LANES), BF16),
        vm((width, 2 * passes * LANES), BF16),
        vm((passes, LANES, width), BF16),
        vm((passes, width, 3 * LANES), BF16),
        vm((passes, LANES, width), BF16),
        vm((passes, width, hidden), BF16),
        vm((passes, hidden, width), BF16),
        vm((passes, frame_count, LANES), BF16),
        vm((passes, LANES + ONES, frame_count), BF16),
        vm((passes, latent_count, LANES), BF16),
        vm((2 * latent_count, LANES), BF16),
        vm((1, 2 * latent_count), F32),
        vm((LANES + ONES, 2 * latent_count), F32),
        vm((passes, latent_count, LANES), BF16),
        vm((passes, latent_count // LANES, 2, LANES), F32),
        vm((passes, nf, rows_each, LANES), BF16),
        vm((passes, nf, 2, LANES), F32),
        vm((LANES, 2 * nf), F32),
        vm((passes, latent_count, LANES), BF16),
        vm((passes, latent_count, LANES), BF16),
        vm((passes, 3, rows_each, width // 2), BF16),
        vm((passes, 3, rows_each, width // 2), BF16),
        vm((passes, 3, nh, rows_each, width // 2), BF16),
        vm((rows_each, width), F32),
        vm((latent_count, LANES), F32),
        pltpu.SemaphoreType.DMA((8,)),
        pltpu.SemaphoreType.DMA((CHUNKS,)),
        pltpu.SemaphoreType.DMA((7, CHUNKS)),
        pltpu.SemaphoreType.DMA(()),
        pltpu.SemaphoreType.DMA((passes, 12)),
        pltpu.SemaphoreType.DMA((passes, 12)),
    ]
    return pl.pallas_call(
        functools.partial(kernel, nf, nh),
        out_shape=(
            jax.ShapeDtypeStruct((rows_each, width), F32),
            jax.ShapeDtypeStruct((latent_count, LANES), F32),
        ),
        in_specs=[pl.BlockSpec(memory_space=pl.ANY)] * len(args),
        out_specs=(pl.BlockSpec(memory_space=vm), pl.BlockSpec(memory_space=vm)),
        scratch_shapes=scratch,
        compiler_params=pltpu.CompilerParams(
            collective_id=0, has_side_effects=True, vmem_limit_bytes=56 * 1024 * 1024
        ),
    )(*args)


def solution(mesh):
    nf, nh = mesh.shape["frames"], mesh.shape["heads"]
    by_column, by_row = P(None, None, "heads"), P(None, "heads", None)
    placed = (
        P("frames", "heads"), P(),
        by_column, by_column, by_column, by_row,
        by_column, by_column, by_column, by_row,
        by_column, by_row,
    )
    return jax.shard_map(
        functools.partial(local, nf, nh),
        mesh=mesh,
        in_specs=placed,
        out_specs=(P("frames", None), P(None, "heads")),
        check_vma=False,
    )
```

```python
import functools

import jax
import jax.numpy as jnp
from jax import lax
from jax.experimental import pallas as pl
from jax.experimental.pallas import tpu as pltpu
from jax.sharding import PartitionSpec as P

EPSILON = 1e-05
HEAD_DIM = 64
MESH = pl.DeviceIdType.MESH
F32 = jnp.float32
BF16 = jnp.bfloat16
CHUNKS = 4
PIECES = 8
AHEAD = 5
LANES = 128
ONES = 16
PART, STAT, KEYS, VALUES, QUERY, MID, CROSS, SELF, MLP = range(9)
PAIRS = 3


def layer_norm(v):
    centre = v - jnp.mean(v, axis=-1, keepdims=True)
    spread = jnp.mean(centre * centre, axis=-1, keepdims=True)
    return centre * lax.rsqrt(spread + EPSILON)


def project(a, b):
    return jnp.dot(a, b, preferred_element_type=F32)


def against(a, b):
    return lax.dot_general(a, b, (((1,), (1,)), ((), ())), preferred_element_type=F32)


def lane(shape):
    return lax.broadcasted_iota(jnp.int32, shape, len(shape) - 1)


def by_head(q):
    first = lane(q.shape) < HEAD_DIM
    zero = jnp.zeros_like(q)
    return jnp.concatenate([jnp.where(first, q, zero), jnp.where(first, zero, q)], axis=0)


def farthest_first(nz, nx):
    steps = [(dz, dx) for dz in range(nz) for dx in range(nx) if dz or dx]
    return sorted(steps, key=lambda s: -(min(s[0], nz - s[0]) + min(s[1], nx - s[1])))


def kernel(
    nf, nh,
    frames, latents, cq, ck, cv, co, sq, sk, sv, so, mi, mo,
    encoded, midway,
    x_s, lat_s, cq_s, ckv_s, co_s, sqkv_s, so_s, mi_s, mo_s,
    k_s, vt_s, qall_s, qh_s, m_s, acc_s, o_s, st_s, po_s, ps_s, tr_s, sk_s, sv_s, give_s, take_s, sum_s, row_s, mid_s,
    w_sem, own_sem, ring_recv, ring_send, recv_sem, send_sem,
):
    f, h = lax.axis_index("frames"), lax.axis_index("heads")
    latent_count, width = lat_s.shape
    frame_count = x_s.shape[0]
    rows_each = latent_count // nf
    chunk = frame_count // CHUNKS
    piece = frame_count // PIECES
    half = width // 2
    passes = cq_s.shape[0]

    sib = h + 1 - 2 * lax.rem(h, 2)
    right, left, opp = lax.rem(h + 2, nh), lax.rem(h + nh - 2, nh), lax.rem(h + 4, nh)

    def cols(who):
        return pl.ds(pl.multiple_of(who * LANES, LANES), LANES)

    own_rows = pl.ds(pl.multiple_of(f * rows_each, rows_each), rows_each)

    barrier = pltpu.get_barrier_semaphore()

    nx = 4
    nz = nf // nx
    z, x = f // nx, lax.rem(f, nx)

    def frames_peers():
        for dz, dx in farthest_first(nz, nx):
            yield lax.rem(z + dz, nz) * nx + lax.rem(x + dx, nx)

    def greet_h(p, _):
        pl.semaphore_signal(barrier, inc=1, device_id=(f, lax.rem(h + p, nh)), device_id_type=MESH)
        return 0

    for t in frames_peers():
        pl.semaphore_signal(barrier, inc=1, device_id=(t, h), device_id_type=MESH)
    lax.fori_loop(1, nh, greet_h, 0)
    def local_copies():
        groups = [
            [(latents, lat_s)],
            [(cq, cq_s)],
            [(w.at[p], ckv_s.at[:, pl.ds((2 * p + i) * LANES, LANES)]) for p in range(passes) for i, w in enumerate((ck, cv))],
            [(co, co_s)],
            [(w, sqkv_s.at[:, :, pl.ds(i * LANES, LANES)]) for i, w in enumerate((sq, sk, sv))],
            [(so, so_s)],
            [(mi, mi_s)],
            [(mo, mo_s)],
        ]
        return groups

    own_block = pltpu.make_async_copy(frames, x_s.at[:, cols(h)], own_sem)
    own_block.start()
    for i, group in enumerate(local_copies()):
        for src, dst in group:
            pltpu.make_async_copy(src, dst, w_sem.at[i]).start()

    def loaded(i, ref):
        pltpu.make_async_copy(ref, ref, w_sem.at[i]).wait()

    pl.semaphore_wait(barrier, nf + nh - 2)

    L, R, O, S_OWN, S_L, S_R, S_O = range(7)

    def ring(kind, k, src, dst, to):
        return pltpu.make_async_remote_copy(
            src, dst, ring_send, ring_recv.at[kind, k], device_id=(f, to), device_id_type=MESH
        )

    def block(k, who):
        return x_s.at[pl.ds(k * piece, piece), cols(who)]

    def arrived(kind, k, who):
        ring(kind, k, block(k, who), block(k, who), sib).wait_recv()

    def pass_on(kind, k, who, to):
        ring(kind, k, block(k, who), block(k, who), to).start()

    def send_own(k):
        src = frames.at[pl.ds(k * piece, piece), :]
        ring(L, k, src, block(k, h), right).start()
        ring(R, k, src, block(k, h), left).start()
        ring(S_OWN, k, src, block(k, h), sib).start()

    for k in range(AHEAD):
        send_own(k)

    loaded(0, lat_s)
    loaded(1, cq_s)
    state = lat_s[...].astype(F32)
    q0 = (project(layer_norm(state).astype(BF16), cq_s[0]) * 0.125).astype(BF16)
    qh_s[...] = by_head(q0)
    rows = lat_s[own_rows, :].astype(F32)
    for p in range(passes):
        vt_s[p, pl.ds(LANES, ONES), :] = jnp.ones((ONES, frame_count), BF16)
    loaded(2, ckv_s)

    def keys_values(k):
        r = pl.ds(k * chunk, chunk)
        normed = layer_norm(x_s[r, :].astype(F32)).astype(BF16)
        both = project(normed, ckv_s[...])
        for p in range(passes):
            k_s[p, r, :] = both[:, 2 * p * LANES:(2 * p + 1) * LANES].astype(BF16)
            value = both[:, (2 * p + 1) * LANES:(2 * p + 2) * LANES]
            vt_s[p, pl.ds(0, LANES), r] = value.T.astype(BF16)

    def attend_start():
        m_s[...] = jnp.full_like(m_s, -jnp.inf)
        acc_s[...] = jnp.zeros_like(acc_s)

    def attend(p, k):
        r = pl.ds(pl.multiple_of(k * chunk, chunk), chunk)
        scores = against(k_s[p, r, :], qh_s[...])
        before = m_s[...]
        highest = jnp.maximum(before, jnp.max(scores, axis=0, keepdims=True))
        terms = jnp.exp(scores - highest).astype(BF16)
        acc_s[...] = acc_s[...] * jnp.exp(before - highest) + project(vt_s[p, :, r], terms)
        m_s[...] = highest

    outstanding = []

    def exchange_f(kind, p, source, there, everything):
        for t in frames_peers():
            pltpu.make_async_remote_copy(
                source(t), there, send_sem.at[p, kind], recv_sem.at[p, kind],
                device_id=(t, h), device_id_type=MESH,
            ).start()
        outstanding.append(lambda: sent(kind, p, everything))

    def landed(kind, p, ref):
        pltpu.make_async_remote_copy(
            ref, ref, send_sem.at[p, kind], recv_sem.at[p, kind], device_id=(f, sib), device_id_type=MESH
        ).wait_recv()

    def sent(kind, p, ref):
        pltpu.make_async_remote_copy(
            ref, ref, send_sem.at[p, kind], recv_sem.at[p, kind], device_id=(f, sib), device_id_type=MESH
        ).wait_send()

    def attend_end(p):
        total = acc_s[pl.ds(LANES, 1), :]
        value = acc_s[pl.ds(0, LANES), :] / total
        both = jnp.concatenate(
            [value[:HEAD_DIM, :latent_count], value[HEAD_DIM:, latent_count:]], axis=0
        )
        o_s[p] = both.T.astype(BF16)
        level = m_s[...] + jnp.log(total)
        for t in range(latent_count // LANES):
            for i in range(2):
                at = i * latent_count + t * LANES
                st_s[p, t, pl.ds(i, 1), :] = level[:, at:at + LANES]

        def rows_of(t):
            return pl.ds(pl.multiple_of(t * rows_each, rows_each), rows_each)

        per_tile = LANES // rows_each
        stats, parts = ps_s.at[p, pl.ds(0, nf - 1)], po_s.at[p, pl.ds(0, nf - 1)]
        exchange_f(STAT, p, lambda t: st_s.at[p, t // per_tile], ps_s.at[p, f], stats)
        exchange_f(PART, p, lambda t: o_s.at[p, rows_of(t), :], po_s.at[p, f], parts)
        po_s[p, f] = o_s[p, own_rows, :]
        ps_s[p, f] = st_s[p, f // per_tile]
        landed(STAT, p, stats)
        levels = jnp.concatenate([ps_s[p, :, 0, :], ps_s[p, :, 1, :]], axis=0)
        tr_s[...] = levels.T
        mine = tr_s[pl.ds(pl.multiple_of(lax.rem(f, per_tile) * rows_each, rows_each), rows_each), :]
        weights = []
        for i in range(2):
            level = mine[:, i * nf:(i + 1) * nf]
            e = jnp.exp(level - jnp.max(level, axis=1, keepdims=True))
            weights.append(e / jnp.sum(e, axis=1, keepdims=True))
        landed(PART, p, parts)
        first = lane((rows_each, LANES)) < HEAD_DIM
        context = jnp.zeros((rows_each, LANES), F32)
        for s in range(nf):
            w = jnp.where(first, weights[0][:, s:s + 1], weights[1][:, s:s + 1])
            context += w * po_s[p, s].astype(F32)
        return context.astype(BF16)

    core = lax.rem(h, 2)

    def half_of(c):
        return pl.ds(pl.multiple_of(c * half, half), half)

    def head_total(kind, slot, p, left_side, weight):
        give_s[p, slot] = project(left_side, weight[p, :, half_of(1 - core)]).astype(BF16)
        pair = pltpu.make_async_remote_copy(
            give_s.at[p, slot], take_s.at[p, slot], send_sem.at[p, kind + PAIRS], recv_sem.at[p, kind + PAIRS],
            device_id=(f, sib), device_id_type=MESH,
        )
        pair.start()
        mine = project(left_side, weight[p, :, half_of(core)])
        pair.wait()
        sum_s[p, slot, h] = (mine + take_s[p, slot].astype(F32)).astype(BF16)
        for d in (4, 5, 3, 2, 6, 7, 1):
            pltpu.make_async_remote_copy(
                sum_s.at[p, slot, h], sum_s.at[p, slot, h], send_sem.at[p, kind], recv_sem.at[p, kind],
                device_id=(f, lax.rem(h + d, nh)), device_id_type=MESH,
            ).start()
        outstanding.append(lambda: sent(kind, p, sum_s.at[p, slot, pl.ds(0, nh - 1)]))
        landed(kind, p, sum_s.at[p, slot, pl.ds(0, nh - 1)])
        halves = []
        for c in range(2):
            out = sum_s[p, slot, c].astype(F32)
            for i in range(c + 2, nh, 2):
                out += sum_s[p, slot, i].astype(F32)
            halves.append(out)
        return jnp.concatenate(halves, axis=1)

    attend_start()

    def neighbours(k):
        onward = ((L, left, right), (R, right, left))[k % 2]
        arrived(L, k, left)
        arrived(R, k, right)
        pass_on(O, k, onward[1], onward[2])
        if k + AHEAD < PIECES:
            send_own(k + AHEAD)
        pass_on(S_L, k, left, sib)
        pass_on(S_R, k, right, sib)

    def opposite(k):
        arrived(O, k, opp)
        pass_on(S_O, k, opp, sib)

    def complete(c):
        per = PIECES // CHUNKS
        for k in range(c * per, (c + 1) * per):
            for kind in (S_OWN, S_L, S_R, S_O):
                arrived(kind, k, sib)
        keys_values(c)
        attend(0, c)

    own_block.wait()
    lag = 4
    for j in range(PIECES + lag):
        if j < PIECES:
            neighbours(j)
        if j >= lag:
            opposite(j - lag)
        done = j - lag - 1
        if done >= 0 and done % 2 == 1:
            complete(done // 2)
    complete(CHUNKS - 1)

    for p in range(passes):
        if p > 0:
            attend_start()
            qh_s[...] = by_head(qall_s[p])

            def again(k, _):
                attend(p, k)
                return 0

            lax.fori_loop(0, CHUNKS, again, 0)
        if p == 1:
            landed(MID, 0, mid_s.at[pl.ds(0, latent_count - rows_each)])
            mid_out = pltpu.make_async_copy(mid_s, midway, own_sem)
            mid_out.start()
        context = attend_end(p)
        if p == 0:
            loaded(3, co_s)
        rows = rows + head_total(CROSS, 0, p, context, co_s)

        if p == 0:
            loaded(4, sqkv_s)
        self_in = layer_norm(rows).astype(BF16)
        others = pl.ds(0, latent_count - rows_each)
        for i, (kind, ref) in enumerate(((KEYS, sk_s), (VALUES, sv_s))):
            ref[p, own_rows, :] = project(self_in, sqkv_s[p, :, pl.ds((i + 1) * LANES, LANES)]).astype(BF16)
            here = ref.at[p, own_rows, :]
            exchange_f(kind, p, lambda t: here, here, ref.at[p, others, :])
        q = by_head((project(self_in, sqkv_s[p, :, pl.ds(0, LANES)]) * 0.125).astype(BF16))
        landed(KEYS, p, sk_s.at[p, others, :])
        scores = against(q, sk_s[p])
        e = jnp.exp(scores - jnp.max(scores, axis=1, keepdims=True))
        weight = (e / jnp.sum(e, axis=1, keepdims=True)).astype(BF16)
        landed(VALUES, p, sv_s.at[p, others, :])
        both = project(weight, sv_s[p])
        first = lane((rows_each, LANES)) < HEAD_DIM
        context = jnp.where(first, both[:rows_each], both[rows_each:]).astype(BF16)
        if p == 0:
            loaded(5, so_s)
        rows = rows + head_total(SELF, 1, p, context, so_s)

        if p == 0:
            loaded(6, mi_s)
        u = project(layer_norm(rows).astype(BF16), mi_s[p])
        hidden = (0.5 * u * (1.0 + lax.erf(u * 0.7071067811865476))).astype(BF16)
        if p == 0:
            loaded(7, mo_s)
        rows = rows + head_total(MLP, 2, p, hidden, mo_s)

        if p + 1 < passes:
            q = (project(layer_norm(rows).astype(BF16), cq_s[p + 1]) * 0.125).astype(BF16)
            qall_s[p + 1, own_rows, :] = q
            here = qall_s.at[p + 1, own_rows, :]
            exchange_f(QUERY, p, lambda t: here, here, qall_s.at[p + 1, others, :])
        if p == 0:
            row_s[...] = rows
            source, there = row_s.at[:, cols(h)], mid_s.at[own_rows, :]
            exchange_f(MID, p, lambda t: source, there, mid_s.at[others, :])
            mid_s[own_rows, :] = row_s[:, cols(h)]
        if p + 1 < passes:
            landed(QUERY, p, qall_s.at[p + 1, others, :])

    encoded[...] = rows
    mid_out.wait()

    ring(0, 0, x_s.at[:, pl.ds(0, 7 * LANES)], x_s.at[:, pl.ds(0, 7 * LANES)], sib).wait_send()
    for wait in outstanding:
        wait()


def hand_over(a, b, a_out, b_out, sem):
    copies = [pltpu.make_async_copy(x, y, sem.at[i]) for i, (x, y) in enumerate(((a, a_out), (b, b_out)))]
    for c in copies:
        c.start()
    for c in copies:
        c.wait()


def local(nf, nh, *args):
    frames, latents, cq, mi = args[0], args[1], args[2], args[10]
    frame_count = frames.shape[0]
    latent_count, width = latents.shape
    passes, hidden = cq.shape[0], mi.shape[2]
    rows_each = latent_count // nf
    vm = pltpu.VMEM
    scratch = [
        vm((frame_count, width), BF16),
        vm((latent_count, width), BF16),
        vm((passes, width, LANES), BF16),
        vm((width, 2 * passes * LANES), BF16),
        vm((passes, LANES, width), BF16),
        vm((passes, width, 3 * LANES), BF16),
        vm((passes, LANES, width), BF16),
        vm((passes, width, hidden), BF16),
        vm((passes, hidden, width), BF16),
        vm((passes, frame_count, LANES), BF16),
        vm((passes, LANES + ONES, frame_count), BF16),
        vm((passes, latent_count, LANES), BF16),
        vm((2 * latent_count, LANES), BF16),
        vm((1, 2 * latent_count), F32),
        vm((LANES + ONES, 2 * latent_count), F32),
        vm((passes, latent_count, LANES), BF16),
        vm((passes, latent_count // LANES, 2, LANES), F32),
        vm((passes, nf, rows_each, LANES), BF16),
        vm((passes, nf, 2, LANES), F32),
        vm((LANES, 2 * nf), F32),
        vm((passes, latent_count, LANES), BF16),
        vm((passes, latent_count, LANES), BF16),
        vm((passes, 3, rows_each, width // 2), BF16),
        vm((passes, 3, rows_each, width // 2), BF16),
        vm((passes, 3, nh, rows_each, width // 2), BF16),
        vm((rows_each, width), F32),
        vm((latent_count, LANES), F32),
        pltpu.SemaphoreType.DMA((8,)),
        pltpu.SemaphoreType.DMA(()),
        pltpu.SemaphoreType.DMA((7, PIECES)),
        pltpu.SemaphoreType.DMA(()),
        pltpu.SemaphoreType.DMA((passes, 12)),
        pltpu.SemaphoreType.DMA((passes, 12)),
    ]
    outs = pl.pallas_call(
        functools.partial(kernel, nf, nh),
        out_shape=(
            jax.ShapeDtypeStruct((rows_each, width), F32),
            jax.ShapeDtypeStruct((latent_count, LANES), F32),
        ),
        in_specs=[pl.BlockSpec(memory_space=pl.ANY)] * len(args),
        out_specs=(pl.BlockSpec(memory_space=vm), pl.BlockSpec(memory_space=pl.ANY)),
        scratch_shapes=scratch,
        compiler_params=pltpu.CompilerParams(
            collective_id=0, has_side_effects=True, vmem_limit_bytes=56 * 1024 * 1024
        ),
    )(*args)
    return pl.pallas_call(
        hand_over,
        out_shape=tuple(jax.ShapeDtypeStruct(a.shape, a.dtype) for a in outs),
        in_specs=[pl.BlockSpec(memory_space=pl.ANY)] * 2,
        out_specs=[pl.BlockSpec(memory_space=pl.ANY)] * 2,
        scratch_shapes=[pltpu.SemaphoreType.DMA((2,))],
    )(*outs)


def solution(mesh):
    nf, nh = mesh.shape["frames"], mesh.shape["heads"]
    by_column, by_row = P(None, None, "heads"), P(None, "heads", None)
    placed = (
        P("frames", "heads"), P(),
        by_column, by_column, by_column, by_row,
        by_column, by_column, by_column, by_row,
        by_column, by_row,
    )
    return jax.shard_map(
        functools.partial(local, nf, nh),
        mesh=mesh,
        in_specs=placed,
        out_specs=(P("frames", None), P(None, "heads")),
        check_vma=False,
    )
```

```python
import functools

import jax
import jax.numpy as jnp
from jax import lax
from jax.experimental import pallas as pl
from jax.experimental.pallas import tpu as pltpu
from jax.sharding import PartitionSpec as P

EPSILON = 1e-05
HEAD_DIM = 64
MESH = pl.DeviceIdType.MESH
F32 = jnp.float32
BF16 = jnp.bfloat16
CHUNKS = 4
LANES = 128
ONES = 16
PART, STAT, KEYS, VALUES, QUERY, MID, CROSS, SELF, MLP = range(9)
PAIRS = 3


def layer_norm(v):
    centre = v - jnp.mean(v, axis=-1, keepdims=True)
    spread = jnp.mean(centre * centre, axis=-1, keepdims=True)
    return centre * lax.rsqrt(spread + EPSILON)


def project(a, b):
    return jnp.dot(a, b, preferred_element_type=F32)


def against(a, b):
    return lax.dot_general(a, b, (((1,), (1,)), ((), ())), preferred_element_type=F32)


def lane(shape):
    return lax.broadcasted_iota(jnp.int32, shape, len(shape) - 1)


def by_head(q):
    first = lane(q.shape) < HEAD_DIM
    zero = jnp.zeros_like(q)
    return jnp.concatenate([jnp.where(first, q, zero), jnp.where(first, zero, q)], axis=0)


def farthest_first(nz, nx):
    steps = [(dz, dx) for dz in range(nz) for dx in range(nx) if dz or dx]
    return sorted(steps, key=lambda s: -(min(s[0], nz - s[0]) + min(s[1], nx - s[1])))


def kernel(
    nf, nh,
    frames, latents, cq, ck, cv, co, sq, sk, sv, so, mi, mo,
    encoded, midway,
    x_s, lat_s, cq_s, ckv_s, co_s, sqkv_s, so_s, mi_s, mo_s,
    k_s, vt_s, qall_s, qh_s, m_s, acc_s, o_s, st_s, po_s, ps_s, tr_s, sk_s, sv_s, give_s, take_s, sum_s, row_s, mid_s,
    w_sem, own_sem, ring_recv, ring_send, recv_sem, send_sem,
):
    f, h = lax.axis_index("frames"), lax.axis_index("heads")
    latent_count, width = lat_s.shape
    frame_count = x_s.shape[0]
    rows_each = latent_count // nf
    chunk = frame_count // CHUNKS
    half = width // 2
    passes = cq_s.shape[0]

    sib = h + 1 - 2 * lax.rem(h, 2)
    right, left, opp = lax.rem(h + 2, nh), lax.rem(h + nh - 2, nh), lax.rem(h + 4, nh)

    def cols(who):
        return pl.ds(pl.multiple_of(who * LANES, LANES), LANES)

    own_rows = pl.ds(pl.multiple_of(f * rows_each, rows_each), rows_each)

    def local_copies():
        groups = [
            [(latents, lat_s)],
            [(cq, cq_s)],
            [(w.at[p], ckv_s.at[:, pl.ds((2 * p + i) * LANES, LANES)]) for p in range(passes) for i, w in enumerate((ck, cv))],
            [(co, co_s)],
            [(w, sqkv_s.at[:, :, pl.ds(i * LANES, LANES)]) for i, w in enumerate((sq, sk, sv))],
            [(so, so_s)],
            [(mi, mi_s)],
            [(mo, mo_s)],
        ]
        return groups

    for k in range(CHUNKS):
        r = pl.ds(k * chunk, chunk)
        pltpu.make_async_copy(frames.at[r, :], x_s.at[r, cols(h)], own_sem.at[k]).start()
    for i, group in enumerate(local_copies()):
        for src, dst in group:
            pltpu.make_async_copy(src, dst, w_sem.at[i]).start()

    def loaded(i, ref):
        pltpu.make_async_copy(ref, ref, w_sem.at[i]).wait()

    barrier = pltpu.get_barrier_semaphore()

    nx = 4
    nz = nf // nx
    z, x = f // nx, lax.rem(f, nx)

    def frames_peers():
        for dz, dx in farthest_first(nz, nx):
            yield lax.rem(z + dz, nz) * nx + lax.rem(x + dx, nx)

    def greet_h(p, _):
        pl.semaphore_signal(barrier, inc=1, device_id=(f, lax.rem(h + p, nh)), device_id_type=MESH)
        return 0

    for t in frames_peers():
        pl.semaphore_signal(barrier, inc=1, device_id=(t, h), device_id_type=MESH)
    lax.fori_loop(1, nh, greet_h, 0)
    pl.semaphore_wait(barrier, nf + nh - 2)

    L, R, O, S_OWN, S_L, S_R, S_O = range(7)

    def ring(kind, k, src, dst, to):
        return pltpu.make_async_remote_copy(
            src, dst, ring_send, ring_recv.at[kind, k], device_id=(f, to), device_id_type=MESH
        )

    def block(k, who):
        return x_s.at[pl.ds(k * chunk, chunk), cols(who)]

    def arrived(kind, k, who):
        ring(kind, k, block(k, who), block(k, who), sib).wait_recv()

    def pass_on(kind, k, who, to):
        ring(kind, k, block(k, who), block(k, who), to).start()

    evens, odds = range(0, CHUNKS, 2), range(1, CHUNKS, 2)
    for a, b in zip((*evens, *odds), (*odds, *evens)):
        for kind, k, to in ((L, a, right), (R, b, left)):
            ring(kind, k, frames.at[pl.ds(k * chunk, chunk), :], block(k, h), to).start()
    for k in range(CHUNKS):
        ring(S_OWN, k, frames.at[pl.ds(k * chunk, chunk), :], block(k, h), sib).start()

    loaded(0, lat_s)
    loaded(1, cq_s)
    state = lat_s[...].astype(F32)
    q0 = (project(layer_norm(state).astype(BF16), cq_s[0]) * 0.125).astype(BF16)
    qh_s[...] = by_head(q0)
    rows = lat_s[own_rows, :].astype(F32)
    for p in range(passes):
        vt_s[p, pl.ds(LANES, ONES), :] = jnp.ones((ONES, frame_count), BF16)
    loaded(2, ckv_s)

    def keys_values(k):
        r = pl.ds(k * chunk, chunk)
        normed = layer_norm(x_s[r, :].astype(F32)).astype(BF16)
        both = project(normed, ckv_s[...])
        for p in range(passes):
            k_s[p, r, :] = both[:, 2 * p * LANES:(2 * p + 1) * LANES].astype(BF16)
            value = both[:, (2 * p + 1) * LANES:(2 * p + 2) * LANES]
            vt_s[p, pl.ds(0, LANES), r] = value.T.astype(BF16)

    def attend_start():
        m_s[...] = jnp.full_like(m_s, -jnp.inf)
        acc_s[...] = jnp.zeros_like(acc_s)

    def attend(p, k):
        r = pl.ds(pl.multiple_of(k * chunk, chunk), chunk)
        scores = against(k_s[p, r, :], qh_s[...])
        before = m_s[...]
        highest = jnp.maximum(before, jnp.max(scores, axis=0, keepdims=True))
        terms = jnp.exp(scores - highest).astype(BF16)
        acc_s[...] = acc_s[...] * jnp.exp(before - highest) + project(vt_s[p, :, r], terms)
        m_s[...] = highest

    outstanding = []

    def exchange_f(kind, p, source, there, everything):
        for t in frames_peers():
            pltpu.make_async_remote_copy(
                source(t), there, send_sem.at[p, kind], recv_sem.at[p, kind],
                device_id=(t, h), device_id_type=MESH,
            ).start()
        outstanding.append(lambda: sent(kind, p, everything))

    def landed(kind, p, ref):
        pltpu.make_async_remote_copy(
            ref, ref, send_sem.at[p, kind], recv_sem.at[p, kind], device_id=(f, sib), device_id_type=MESH
        ).wait_recv()

    def sent(kind, p, ref):
        pltpu.make_async_remote_copy(
            ref, ref, send_sem.at[p, kind], recv_sem.at[p, kind], device_id=(f, sib), device_id_type=MESH
        ).wait_send()

    def attend_end(p):
        total = acc_s[pl.ds(LANES, 1), :]
        value = acc_s[pl.ds(0, LANES), :] / total
        both = jnp.concatenate(
            [value[:HEAD_DIM, :latent_count], value[HEAD_DIM:, latent_count:]], axis=0
        )
        o_s[p] = both.T.astype(BF16)
        level = m_s[...] + jnp.log(total)
        for t in range(latent_count // LANES):
            for i in range(2):
                at = i * latent_count + t * LANES
                st_s[p, t, pl.ds(i, 1), :] = level[:, at:at + LANES]

        def rows_of(t):
            return pl.ds(pl.multiple_of(t * rows_each, rows_each), rows_each)

        per_tile = LANES // rows_each
        stats, parts = ps_s.at[p, pl.ds(0, nf - 1)], po_s.at[p, pl.ds(0, nf - 1)]
        exchange_f(STAT, p, lambda t: st_s.at[p, t // per_tile], ps_s.at[p, f], stats)
        exchange_f(PART, p, lambda t: o_s.at[p, rows_of(t), :], po_s.at[p, f], parts)
        po_s[p, f] = o_s[p, own_rows, :]
        ps_s[p, f] = st_s[p, f // per_tile]
        landed(STAT, p, stats)
        levels = jnp.concatenate([ps_s[p, :, 0, :], ps_s[p, :, 1, :]], axis=0)
        tr_s[...] = levels.T
        mine = tr_s[pl.ds(pl.multiple_of(lax.rem(f, per_tile) * rows_each, rows_each), rows_each), :]
        weights = []
        for i in range(2):
            level = mine[:, i * nf:(i + 1) * nf]
            e = jnp.exp(level - jnp.max(level, axis=1, keepdims=True))
            weights.append(e / jnp.sum(e, axis=1, keepdims=True))
        landed(PART, p, parts)
        first = lane((rows_each, LANES)) < HEAD_DIM
        context = jnp.zeros((rows_each, LANES), F32)
        for s in range(nf):
            w = jnp.where(first, weights[0][:, s:s + 1], weights[1][:, s:s + 1])
            context += w * po_s[p, s].astype(F32)
        return context.astype(BF16)

    core = lax.rem(h, 2)

    def half_of(c):
        return pl.ds(pl.multiple_of(c * half, half), half)

    def send_midway():
        source, there = row_s.at[:, cols(h)], mid_s.at[own_rows, :]
        exchange_f(MID, 0, lambda t: source, there, mid_s.at[pl.ds(0, latent_count - rows_each), :])
        mid_s[own_rows, :] = row_s[:, cols(h)]

    def head_total(kind, slot, p, left_side, weight, meanwhile=None):
        give_s[p, slot] = project(left_side, weight[p, :, half_of(1 - core)]).astype(BF16)
        pair = pltpu.make_async_remote_copy(
            give_s.at[p, slot], take_s.at[p, slot], send_sem.at[p, kind + PAIRS], recv_sem.at[p, kind + PAIRS],
            device_id=(f, sib), device_id_type=MESH,
        )
        pair.start()
        mine = project(left_side, weight[p, :, half_of(core)])
        pair.wait()
        sum_s[p, slot, h] = (mine + take_s[p, slot].astype(F32)).astype(BF16)
        for d in (4, 5, 3, 2, 6, 7, 1):
            pltpu.make_async_remote_copy(
                sum_s.at[p, slot, h], sum_s.at[p, slot, h], send_sem.at[p, kind], recv_sem.at[p, kind],
                device_id=(f, lax.rem(h + d, nh)), device_id_type=MESH,
            ).start()
        outstanding.append(lambda: sent(kind, p, sum_s.at[p, slot, pl.ds(0, nh - 1)]))
        if meanwhile is not None:
            meanwhile()
        landed(kind, p, sum_s.at[p, slot, pl.ds(0, nh - 1)])
        halves = []
        for c in range(2):
            out = sum_s[p, slot, c].astype(F32)
            for i in range(c + 2, nh, 2):
                out += sum_s[p, slot, i].astype(F32)
            halves.append(out)
        return jnp.concatenate(halves, axis=1)

    attend_start()

    for k in range(CHUNKS):
        kind, onward, who, to = (L, S_L, left, right) if k % 2 == 0 else (R, S_R, right, left)
        arrived(kind, k, who)
        pass_on(O, k, who, to)
        pass_on(onward, k, who, sib)
    for k in (*odds, *evens):
        kind, onward, who = (R, S_R, right) if k % 2 == 0 else (L, S_L, left)
        arrived(kind, k, who)
        pass_on(onward, k, who, sib)
    for j in range(CHUNKS + 1):
        if j < CHUNKS:
            arrived(O, j, opp)
            pass_on(S_O, j, opp, sib)
        if j > 0:
            k = j - 1
            r = pl.ds(k * chunk, chunk)
            pltpu.make_async_copy(frames.at[r, :], x_s.at[r, cols(h)], own_sem.at[k]).wait()
            for kind in (S_OWN, S_L, S_R, S_O):
                arrived(kind, k, sib)
            keys_values(k)
            attend(0, k)

    for p in range(passes):
        if p > 0:
            attend_start()
            qh_s[...] = by_head(qall_s[p])

            def again(k, _):
                attend(p, k)
                return 0

            lax.fori_loop(0, CHUNKS, again, 0)
        context = attend_end(p)
        if p == 0:
            loaded(3, co_s)
        rows = rows + head_total(CROSS, 0, p, context, co_s)

        if p == 0:
            loaded(4, sqkv_s)
        self_in = layer_norm(rows).astype(BF16)
        others = pl.ds(0, latent_count - rows_each)
        for i, (kind, ref) in enumerate(((KEYS, sk_s), (VALUES, sv_s))):
            ref[p, own_rows, :] = project(self_in, sqkv_s[p, :, pl.ds((i + 1) * LANES, LANES)]).astype(BF16)
            here = ref.at[p, own_rows, :]
            exchange_f(kind, p, lambda t: here, here, ref.at[p, others, :])
        q = by_head((project(self_in, sqkv_s[p, :, pl.ds(0, LANES)]) * 0.125).astype(BF16))
        landed(KEYS, p, sk_s.at[p, others, :])
        scores = against(q, sk_s[p])
        e = jnp.exp(scores - jnp.max(scores, axis=1, keepdims=True))
        weight = (e / jnp.sum(e, axis=1, keepdims=True)).astype(BF16)
        landed(VALUES, p, sv_s.at[p, others, :])
        both = project(weight, sv_s[p])
        first = lane((rows_each, LANES)) < HEAD_DIM
        context = jnp.where(first, both[:rows_each], both[rows_each:]).astype(BF16)
        if p == 0:
            loaded(5, so_s)
        rows = rows + head_total(SELF, 1, p, context, so_s, send_midway if p == 1 else None)

        if p == 0:
            loaded(6, mi_s)
        u = project(layer_norm(rows).astype(BF16), mi_s[p])
        hidden = (0.5 * u * (1.0 + lax.erf(u * 0.7071067811865476))).astype(BF16)
        if p == 0:
            loaded(7, mo_s)
        rows = rows + head_total(MLP, 2, p, hidden, mo_s)

        if p + 1 < passes:
            q = (project(layer_norm(rows).astype(BF16), cq_s[p + 1]) * 0.125).astype(BF16)
            qall_s[p + 1, own_rows, :] = q
            here = qall_s.at[p + 1, own_rows, :]
            exchange_f(QUERY, p, lambda t: here, here, qall_s.at[p + 1, others, :])
        if p == 0:
            row_s[...] = rows
        if p + 1 < passes:
            landed(QUERY, p, qall_s.at[p + 1, others, :])

    encoded[...] = rows
    landed(MID, 0, mid_s.at[pl.ds(0, latent_count - rows_each)])
    midway[...] = mid_s[...]

    ring(0, 0, x_s.at[:, pl.ds(0, 7 * LANES)], x_s.at[:, pl.ds(0, 7 * LANES)], sib).wait_send()
    for wait in outstanding:
        wait()


def hand_over(a, b, a_out, b_out):
    a_out[...] = a[...]
    b_out[...] = b[...]


def local(nf, nh, *args):
    frames, latents, cq, mi = args[0], args[1], args[2], args[10]
    frame_count = frames.shape[0]
    latent_count, width = latents.shape
    passes, hidden = cq.shape[0], mi.shape[2]
    rows_each = latent_count // nf
    vm = pltpu.VMEM
    scratch = [
        vm((frame_count, width), BF16),
        vm((latent_count, width), BF16),
        vm((passes, width, LANES), BF16),
        vm((width, 2 * passes * LANES), BF16),
        vm((passes, LANES, width), BF16),
        vm((passes, width, 3 * LANES), BF16),
        vm((passes, LANES, width), BF16),
        vm((passes, width, hidden), BF16),
        vm((passes, hidden, width), BF16),
        vm((passes, frame_count, LANES), BF16),
        vm((passes, LANES + ONES, frame_count), BF16),
        vm((passes, latent_count, LANES), BF16),
        vm((2 * latent_count, LANES), BF16),
        vm((1, 2 * latent_count), F32),
        vm((LANES + ONES, 2 * latent_count), F32),
        vm((passes, latent_count, LANES), BF16),
        vm((passes, latent_count // LANES, 2, LANES), F32),
        vm((passes, nf, rows_each, LANES), BF16),
        vm((passes, nf, 2, LANES), F32),
        vm((LANES, 2 * nf), F32),
        vm((passes, latent_count, LANES), BF16),
        vm((passes, latent_count, LANES), BF16),
        vm((passes, 3, rows_each, width // 2), BF16),
        vm((passes, 3, rows_each, width // 2), BF16),
        vm((passes, 3, nh, rows_each, width // 2), BF16),
        vm((rows_each, width), F32),
        vm((latent_count, LANES), F32),
        pltpu.SemaphoreType.DMA((8,)),
        pltpu.SemaphoreType.DMA((CHUNKS,)),
        pltpu.SemaphoreType.DMA((7, CHUNKS)),
        pltpu.SemaphoreType.DMA(()),
        pltpu.SemaphoreType.DMA((passes, 12)),
        pltpu.SemaphoreType.DMA((passes, 12)),
    ]
    outs = pl.pallas_call(
        functools.partial(kernel, nf, nh),
        out_shape=(
            jax.ShapeDtypeStruct((rows_each, width), F32),
            jax.ShapeDtypeStruct((latent_count, LANES), F32),
        ),
        in_specs=[pl.BlockSpec(memory_space=pl.ANY)] * len(args),
        out_specs=(pl.BlockSpec(memory_space=vm), pl.BlockSpec(memory_space=vm)),
        scratch_shapes=scratch,
        compiler_params=pltpu.CompilerParams(
            collective_id=0, has_side_effects=True, vmem_limit_bytes=56 * 1024 * 1024
        ),
    )(*args)
    return pl.pallas_call(
        hand_over,
        out_shape=tuple(jax.ShapeDtypeStruct(a.shape, a.dtype) for a in outs),
        in_specs=[pl.BlockSpec(memory_space=vm)] * 2,
        out_specs=[pl.BlockSpec(memory_space=vm)] * 2,
    )(*outs)


def solution(mesh):
    nf, nh = mesh.shape["frames"], mesh.shape["heads"]
    by_column, by_row = P(None, None, "heads"), P(None, "heads", None)
    placed = (
        P("frames", "heads"), P(),
        by_column, by_column, by_column, by_row,
        by_column, by_column, by_column, by_row,
        by_column, by_row,
    )
    return jax.shard_map(
        functools.partial(local, nf, nh),
        mesh=mesh,
        in_specs=placed,
        out_specs=(P("frames", None), P(None, "heads")),
        check_vma=False,
    )
```

```python
import functools

import jax
import jax.numpy as jnp
from jax import lax
from jax.experimental import pallas as pl
from jax.experimental.pallas import tpu as pltpu
from jax.sharding import PartitionSpec as P

EPSILON = 1e-05
HEAD_DIM = 64
MESH = pl.DeviceIdType.MESH
F32 = jnp.float32
BF16 = jnp.bfloat16
CHUNKS = 4
LANES = 128
ONES = 16
PART, STAT, KEYS, VALUES, QUERY, MID, CROSS, SELF, MLP = range(9)
PAIRS = 3


def layer_norm(v):
    centre = v - jnp.mean(v, axis=-1, keepdims=True)
    spread = jnp.mean(centre * centre, axis=-1, keepdims=True)
    return centre * lax.rsqrt(spread + EPSILON)


def project(a, b):
    return jnp.dot(a, b, preferred_element_type=F32)


def against(a, b):
    return lax.dot_general(a, b, (((1,), (1,)), ((), ())), preferred_element_type=F32)


def lane(shape):
    return lax.broadcasted_iota(jnp.int32, shape, len(shape) - 1)


def by_head(q):
    first = lane(q.shape) < HEAD_DIM
    zero = jnp.zeros_like(q)
    return jnp.concatenate([jnp.where(first, q, zero), jnp.where(first, zero, q)], axis=0)


def farthest_first(nz, nx):
    steps = [(dz, dx) for dz in range(nz) for dx in range(nx) if dz or dx]
    return sorted(steps, key=lambda s: -(min(s[0], nz - s[0]) + min(s[1], nx - s[1])))


def kernel(
    nf, nh,
    frames, latents, cq, ck, cv, co, sq, sk, sv, so, mi, mo,
    encoded, midway,
    x_s, xn_s, lat_s, cq_s, ckv_s, co_s, sqkv_s, so_s, mi_s, mo_s,
    k_s, vt_s, qall_s, qh_s, m_s, acc_s, o_s, st_s, po_s, ps_s, tr_s, sk_s, sv_s, give_s, take_s, sum_s, row_s, mid_s,
    w_sem, own_sem, ring_recv, ring_send, recv_sem, send_sem,
):
    f, h = lax.axis_index("frames"), lax.axis_index("heads")
    latent_count, width = lat_s.shape
    frame_count = x_s.shape[0]
    rows_each = latent_count // nf
    chunk = frame_count // CHUNKS
    half = width // 2
    passes = cq_s.shape[0]

    sib = h + 1 - 2 * lax.rem(h, 2)
    right, left, opp = lax.rem(h + 2, nh), lax.rem(h + nh - 2, nh), lax.rem(h + 4, nh)

    def cols(who):
        return pl.ds(pl.multiple_of(who * LANES, LANES), LANES)

    own_rows = pl.ds(pl.multiple_of(f * rows_each, rows_each), rows_each)

    def local_copies():
        groups = [
            [(latents, lat_s)],
            [(cq, cq_s)],
            [(w.at[p], ckv_s.at[:, pl.ds((2 * p + i) * LANES, LANES)]) for p in range(passes) for i, w in enumerate((ck, cv))],
            [(co, co_s)],
            [(w, sqkv_s.at[:, :, pl.ds(i * LANES, LANES)]) for i, w in enumerate((sq, sk, sv))],
            [(so, so_s)],
            [(mi, mi_s)],
            [(mo, mo_s)],
        ]
        return groups

    for k in range(CHUNKS):
        r = pl.ds(k * chunk, chunk)
        pltpu.make_async_copy(frames.at[r, :], x_s.at[r, cols(h)], own_sem.at[k]).start()
    for i, group in enumerate(local_copies()):
        for src, dst in group:
            pltpu.make_async_copy(src, dst, w_sem.at[i]).start()

    def loaded(i, ref):
        pltpu.make_async_copy(ref, ref, w_sem.at[i]).wait()

    barrier = pltpu.get_barrier_semaphore()

    nx = 4
    nz = nf // nx
    z, x = f // nx, lax.rem(f, nx)

    def frames_peers():
        for dz, dx in farthest_first(nz, nx):
            yield lax.rem(z + dz, nz) * nx + lax.rem(x + dx, nx)

    def greet_h(p, _):
        pl.semaphore_signal(barrier, inc=1, device_id=(f, lax.rem(h + p, nh)), device_id_type=MESH)
        return 0

    for t in frames_peers():
        pl.semaphore_signal(barrier, inc=1, device_id=(t, h), device_id_type=MESH)
    lax.fori_loop(1, nh, greet_h, 0)
    pl.semaphore_wait(barrier, nf + nh - 2)

    L, R, O, S_OWN, S_L, S_R, S_O = range(7)

    def ring(kind, k, src, dst, to):
        return pltpu.make_async_remote_copy(
            src, dst, ring_send, ring_recv.at[kind, k], device_id=(f, to), device_id_type=MESH
        )

    def block(k, who):
        return x_s.at[pl.ds(k * chunk, chunk), cols(who)]

    def arrived(kind, k, who):
        ring(kind, k, block(k, who), block(k, who), sib).wait_recv()

    def pass_on(kind, k, who, to):
        ring(kind, k, block(k, who), block(k, who), to).start()

    evens, odds = range(0, CHUNKS, 2), range(1, CHUNKS, 2)
    for a, b in zip((*evens, *odds), (*odds, *evens)):
        for kind, k, to in ((L, a, right), (R, b, left)):
            ring(kind, k, frames.at[pl.ds(k * chunk, chunk), :], block(k, h), to).start()
    for k in range(CHUNKS):
        ring(S_OWN, k, frames.at[pl.ds(k * chunk, chunk), :], block(k, h), sib).start()

    loaded(0, lat_s)
    loaded(1, cq_s)
    state = lat_s[...].astype(F32)
    q0 = (project(layer_norm(state).astype(BF16), cq_s[0]) * 0.125).astype(BF16)
    qh_s[...] = by_head(q0)
    rows = lat_s[own_rows, :].astype(F32)
    for p in range(passes):
        vt_s[p, pl.ds(LANES, ONES), :] = jnp.ones((ONES, frame_count), BF16)
    loaded(2, ckv_s)

    def normalise(k):
        r = pl.ds(k * chunk, chunk)
        xn_s[r, :] = layer_norm(x_s[r, :].astype(F32)).astype(BF16)

    def keys_values(p, k):
        r = pl.ds(pl.multiple_of(k * chunk, chunk), chunk)
        both = project(xn_s[r, :], ckv_s[:, pl.ds(2 * p * LANES, 2 * LANES)])
        k_s[p, r, :] = both[:, :LANES].astype(BF16)
        vt_s[p, pl.ds(0, LANES), r] = both[:, LANES:].T.astype(BF16)

    def attend(p):
        scores = against(k_s[p], qh_s[...])
        highest = jnp.max(scores, axis=0, keepdims=True)
        m_s[...] = highest
        acc_s[...] = project(vt_s[p], jnp.exp(scores - highest).astype(BF16))

    outstanding = []

    def exchange_f(kind, p, source, there, everything):
        for t in frames_peers():
            pltpu.make_async_remote_copy(
                source(t), there, send_sem.at[p, kind], recv_sem.at[p, kind],
                device_id=(t, h), device_id_type=MESH,
            ).start()
        outstanding.append(lambda: sent(kind, p, everything))

    def landed(kind, p, ref):
        pltpu.make_async_remote_copy(
            ref, ref, send_sem.at[p, kind], recv_sem.at[p, kind], device_id=(f, sib), device_id_type=MESH
        ).wait_recv()

    def sent(kind, p, ref):
        pltpu.make_async_remote_copy(
            ref, ref, send_sem.at[p, kind], recv_sem.at[p, kind], device_id=(f, sib), device_id_type=MESH
        ).wait_send()

    def attend_end(p):
        total = acc_s[pl.ds(LANES, 1), :]
        value = acc_s[pl.ds(0, LANES), :] / total
        both = jnp.concatenate(
            [value[:HEAD_DIM, :latent_count], value[HEAD_DIM:, latent_count:]], axis=0
        )
        o_s[p] = both.T.astype(BF16)
        level = m_s[...] + jnp.log(total)
        for t in range(latent_count // LANES):
            for i in range(2):
                at = i * latent_count + t * LANES
                st_s[p, t, pl.ds(i, 1), :] = level[:, at:at + LANES]

        def rows_of(t):
            return pl.ds(pl.multiple_of(t * rows_each, rows_each), rows_each)

        per_tile = LANES // rows_each
        stats, parts = ps_s.at[p, pl.ds(0, nf - 1)], po_s.at[p, pl.ds(0, nf - 1)]
        exchange_f(STAT, p, lambda t: st_s.at[p, t // per_tile], ps_s.at[p, f], stats)
        exchange_f(PART, p, lambda t: o_s.at[p, rows_of(t), :], po_s.at[p, f], parts)
        po_s[p, f] = o_s[p, own_rows, :]
        ps_s[p, f] = st_s[p, f // per_tile]
        if p + 1 < passes:
            def later(k, _):
                keys_values(p + 1, k)
                return 0

            lax.fori_loop(0, CHUNKS, later, 0)
        landed(STAT, p, stats)
        levels = jnp.concatenate([ps_s[p, :, 0, :], ps_s[p, :, 1, :]], axis=0)
        tr_s[...] = levels.T
        mine = tr_s[pl.ds(pl.multiple_of(lax.rem(f, per_tile) * rows_each, rows_each), rows_each), :]
        weights = []
        for i in range(2):
            level = mine[:, i * nf:(i + 1) * nf]
            e = jnp.exp(level - jnp.max(level, axis=1, keepdims=True))
            weights.append(e / jnp.sum(e, axis=1, keepdims=True))
        landed(PART, p, parts)
        first = lane((rows_each, LANES)) < HEAD_DIM
        context = jnp.zeros((rows_each, LANES), F32)
        for s in range(nf):
            w = jnp.where(first, weights[0][:, s:s + 1], weights[1][:, s:s + 1])
            context += w * po_s[p, s].astype(F32)
        return context.astype(BF16)

    core = lax.rem(h, 2)

    def half_of(c):
        return pl.ds(pl.multiple_of(c * half, half), half)

    def send_midway():
        source, there = row_s.at[:, cols(h)], mid_s.at[own_rows, :]
        exchange_f(MID, 0, lambda t: source, there, mid_s.at[pl.ds(0, latent_count - rows_each), :])
        mid_s[own_rows, :] = row_s[:, cols(h)]

    midway_copy = pltpu.make_async_copy(mid_s, midway, own_sem.at[0])

    def hand_midway():
        landed(MID, 0, mid_s.at[pl.ds(0, latent_count - rows_each)])
        midway_copy.start()

    def head_total(kind, slot, p, left_side, weight, meanwhile=None):
        give_s[p, slot] = project(left_side, weight[p, :, half_of(1 - core)]).astype(BF16)
        pair = pltpu.make_async_remote_copy(
            give_s.at[p, slot], take_s.at[p, slot], send_sem.at[p, kind + PAIRS], recv_sem.at[p, kind + PAIRS],
            device_id=(f, sib), device_id_type=MESH,
        )
        pair.start()
        mine = project(left_side, weight[p, :, half_of(core)])
        pair.wait()
        sum_s[p, slot, h] = (mine + take_s[p, slot].astype(F32)).astype(BF16)
        for d in (4, 5, 3, 2, 6, 7, 1):
            pltpu.make_async_remote_copy(
                sum_s.at[p, slot, h], sum_s.at[p, slot, h], send_sem.at[p, kind], recv_sem.at[p, kind],
                device_id=(f, lax.rem(h + d, nh)), device_id_type=MESH,
            ).start()
        outstanding.append(lambda: sent(kind, p, sum_s.at[p, slot, pl.ds(0, nh - 1)]))
        if meanwhile is not None:
            meanwhile()
        landed(kind, p, sum_s.at[p, slot, pl.ds(0, nh - 1)])
        halves = []
        for c in range(2):
            out = sum_s[p, slot, c].astype(F32)
            for i in range(c + 2, nh, 2):
                out += sum_s[p, slot, i].astype(F32)
            halves.append(out)
        return jnp.concatenate(halves, axis=1)

    for k in range(CHUNKS):
        kind, onward, who, to = (L, S_L, left, right) if k % 2 == 0 else (R, S_R, right, left)
        arrived(kind, k, who)
        pass_on(O, k, who, to)
        pass_on(onward, k, who, sib)
    for k in (*odds, *evens):
        kind, onward, who = (R, S_R, right) if k % 2 == 0 else (L, S_L, left)
        arrived(kind, k, who)
        pass_on(onward, k, who, sib)
    for j in range(CHUNKS + 1):
        if j < CHUNKS:
            arrived(O, j, opp)
            pass_on(S_O, j, opp, sib)
        if j > 0:
            k = j - 1
            r = pl.ds(k * chunk, chunk)
            pltpu.make_async_copy(frames.at[r, :], x_s.at[r, cols(h)], own_sem.at[k]).wait()
            for kind in (S_OWN, S_L, S_R, S_O):
                arrived(kind, k, sib)
            normalise(k)
            keys_values(0, k)

    for p in range(passes):
        if p > 0:
            qh_s[...] = by_head(qall_s[p])
        attend(p)
        context = attend_end(p)
        if p == 0:
            loaded(3, co_s)
        rows = rows + head_total(CROSS, 0, p, context, co_s)

        if p == 0:
            loaded(4, sqkv_s)
        self_in = layer_norm(rows).astype(BF16)
        others = pl.ds(0, latent_count - rows_each)
        kv = project(self_in, sqkv_s[p, :, pl.ds(LANES, 2 * LANES)])
        for i, (kind, ref) in enumerate(((KEYS, sk_s), (VALUES, sv_s))):
            ref[p, own_rows, :] = kv[:, i * LANES:(i + 1) * LANES].astype(BF16)
            here = ref.at[p, own_rows, :]
            exchange_f(kind, p, lambda t: here, here, ref.at[p, others, :])
        q = by_head((project(self_in, sqkv_s[p, :, pl.ds(0, LANES)]) * 0.125).astype(BF16))
        landed(KEYS, p, sk_s.at[p, others, :])
        scores = against(q, sk_s[p])
        e = jnp.exp(scores - jnp.max(scores, axis=1, keepdims=True))
        weight = (e / jnp.sum(e, axis=1, keepdims=True)).astype(BF16)
        landed(VALUES, p, sv_s.at[p, others, :])
        both = project(weight, sv_s[p])
        first = lane((rows_each, LANES)) < HEAD_DIM
        context = jnp.where(first, both[:rows_each], both[rows_each:]).astype(BF16)
        if p == 0:
            loaded(5, so_s)
        rows = rows + head_total(SELF, 1, p, context, so_s, send_midway if p == 1 else None)

        if p == 0:
            loaded(6, mi_s)
        u = project(layer_norm(rows).astype(BF16), mi_s[p])
        hidden = (0.5 * u * (1.0 + lax.erf(u * 0.7071067811865476))).astype(BF16)
        if p == 0:
            loaded(7, mo_s)
        rows = rows + head_total(MLP, 2, p, hidden, mo_s, hand_midway if p == 1 else None)

        if p + 1 < passes:
            q = (project(layer_norm(rows).astype(BF16), cq_s[p + 1]) * 0.125).astype(BF16)
            qall_s[p + 1, own_rows, :] = q
            here = qall_s.at[p + 1, own_rows, :]
            exchange_f(QUERY, p, lambda t: here, here, qall_s.at[p + 1, others, :])
        if p == 0:
            row_s[...] = rows
        if p + 1 < passes:
            landed(QUERY, p, qall_s.at[p + 1, others, :])

    encoded[...] = rows
    midway_copy.wait()

    ring(0, 0, x_s.at[:, pl.ds(0, 7 * LANES)], x_s.at[:, pl.ds(0, 7 * LANES)], sib).wait_send()
    for wait in outstanding:
        wait()


def hand_over(a, b, a_out, b_out):
    a_out[...] = a[...]
    b_out[...] = b[...]


def local(nf, nh, *args):
    frames, latents, cq, mi = args[0], args[1], args[2], args[10]
    frame_count = frames.shape[0]
    latent_count, width = latents.shape
    passes, hidden = cq.shape[0], mi.shape[2]
    rows_each = latent_count // nf
    vm = pltpu.VMEM
    scratch = [
        vm((frame_count, width), BF16),
        vm((frame_count, width), BF16),
        vm((latent_count, width), BF16),
        vm((passes, width, LANES), BF16),
        vm((width, 2 * passes * LANES), BF16),
        vm((passes, LANES, width), BF16),
        vm((passes, width, 3 * LANES), BF16),
        vm((passes, LANES, width), BF16),
        vm((passes, width, hidden), BF16),
        vm((passes, hidden, width), BF16),
        vm((passes, frame_count, LANES), BF16),
        vm((passes, LANES + ONES, frame_count), BF16),
        vm((passes, latent_count, LANES), BF16),
        vm((2 * latent_count, LANES), BF16),
        vm((1, 2 * latent_count), F32),
        vm((LANES + ONES, 2 * latent_count), F32),
        vm((passes, latent_count, LANES), BF16),
        vm((passes, latent_count // LANES, 2, LANES), F32),
        vm((passes, nf, rows_each, LANES), BF16),
        vm((passes, nf, 2, LANES), F32),
        vm((LANES, 2 * nf), F32),
        vm((passes, latent_count, LANES), BF16),
        vm((passes, latent_count, LANES), BF16),
        vm((passes, 3, rows_each, width // 2), BF16),
        vm((passes, 3, rows_each, width // 2), BF16),
        vm((passes, 3, nh, rows_each, width // 2), BF16),
        vm((rows_each, width), F32),
        vm((latent_count, LANES), F32),
        pltpu.SemaphoreType.DMA((8,)),
        pltpu.SemaphoreType.DMA((CHUNKS,)),
        pltpu.SemaphoreType.DMA((7, CHUNKS)),
        pltpu.SemaphoreType.DMA(()),
        pltpu.SemaphoreType.DMA((passes, 12)),
        pltpu.SemaphoreType.DMA((passes, 12)),
    ]
    outs = pl.pallas_call(
        functools.partial(kernel, nf, nh),
        out_shape=(
            jax.ShapeDtypeStruct((rows_each, width), F32),
            jax.ShapeDtypeStruct((latent_count, LANES), F32),
        ),
        in_specs=[pl.BlockSpec(memory_space=pl.ANY)] * len(args),
        out_specs=(pl.BlockSpec(memory_space=vm), pl.BlockSpec(memory_space=pl.ANY)),
        scratch_shapes=scratch,
        compiler_params=pltpu.CompilerParams(
            collective_id=0, has_side_effects=True, vmem_limit_bytes=56 * 1024 * 1024
        ),
    )(*args)
    return pl.pallas_call(
        hand_over,
        out_shape=tuple(jax.ShapeDtypeStruct(a.shape, a.dtype) for a in outs),
        in_specs=[pl.BlockSpec(memory_space=vm)] * 2,
        out_specs=[pl.BlockSpec(memory_space=vm)] * 2,
    )(*outs)


def solution(mesh):
    nf, nh = mesh.shape["frames"], mesh.shape["heads"]
    by_column, by_row = P(None, None, "heads"), P(None, "heads", None)
    placed = (
        P("frames", "heads"), P(),
        by_column, by_column, by_column, by_row,
        by_column, by_column, by_column, by_row,
        by_column, by_row,
    )
    return jax.shard_map(
        functools.partial(local, nf, nh),
        mesh=mesh,
        in_specs=placed,
        out_specs=(P("frames", None), P(None, "heads")),
        check_vma=False,
    )
```

```python
import functools

import jax
import jax.numpy as jnp
from jax import lax
from jax.experimental import pallas as pl
from jax.experimental.pallas import tpu as pltpu
from jax.sharding import PartitionSpec as P

EPSILON = 1e-05
HEAD_DIM = 64
MESH = pl.DeviceIdType.MESH
F32 = jnp.float32
BF16 = jnp.bfloat16
CHUNKS = 4
LANES = 128
ONES = 16
PART, STAT, KEYS, VALUES, QUERY, MID, CROSS, SELF, MLP = range(9)
PAIRS = 3


def layer_norm(v):
    centre = v - jnp.mean(v, axis=-1, keepdims=True)
    spread = jnp.mean(centre * centre, axis=-1, keepdims=True)
    return centre * lax.rsqrt(spread + EPSILON)


def project(a, b):
    return jnp.dot(a, b, preferred_element_type=F32)


def against(a, b):
    return lax.dot_general(a, b, (((1,), (1,)), ((), ())), preferred_element_type=F32)


def lane(shape):
    return lax.broadcasted_iota(jnp.int32, shape, len(shape) - 1)


def by_head(q):
    first = lane(q.shape) < HEAD_DIM
    zero = jnp.zeros_like(q)
    return jnp.concatenate([jnp.where(first, q, zero), jnp.where(first, zero, q)], axis=0)


def farthest_first(nz, nx):
    steps = [(dz, dx) for dz in range(nz) for dx in range(nx) if dz or dx]
    return sorted(steps, key=lambda s: -(min(s[0], nz - s[0]) + min(s[1], nx - s[1])))


def kernel(
    nf, nh,
    frames, latents, cq, ck, cv, co, sq, sk, sv, so, mi, mo,
    encoded, midway,
    x_s, xn_s, lat_s, cq_s, ckv_s, co_s, sqkv_s, so_s, mi_s, mo_s,
    k_s, vt_s, qall_s, qh_s, m_s, acc_s, o_s, st_s, po_s, ps_s, tr_s, sk_s, sv_s, give_s, take_s, sum_s, row_s, mid_s,
    w_sem, own_sem, ring_recv, ring_send, recv_sem, send_sem,
):
    f, h = lax.axis_index("frames"), lax.axis_index("heads")
    latent_count, width = lat_s.shape
    frame_count = x_s.shape[0]
    rows_each = latent_count // nf
    chunk = frame_count // CHUNKS
    half = width // 2
    passes = cq_s.shape[0]

    sib = h + 1 - 2 * lax.rem(h, 2)
    right, left, opp = lax.rem(h + 2, nh), lax.rem(h + nh - 2, nh), lax.rem(h + 4, nh)

    def cols(who):
        return pl.ds(pl.multiple_of(who * LANES, LANES), LANES)

    own_rows = pl.ds(pl.multiple_of(f * rows_each, rows_each), rows_each)

    def local_copies():
        groups = [
            [(latents, lat_s)],
            [(cq, cq_s)],
            [(w.at[p], ckv_s.at[:, pl.ds((2 * p + i) * LANES, LANES)]) for p in range(passes) for i, w in enumerate((ck, cv))],
            [(co, co_s)],
            [(w, sqkv_s.at[:, :, pl.ds(i * LANES, LANES)]) for i, w in enumerate((sq, sk, sv))],
            [(so, so_s)],
            [(mi, mi_s)],
            [(mo, mo_s)],
        ]
        return groups

    for k in range(CHUNKS):
        r = pl.ds(k * chunk, chunk)
        pltpu.make_async_copy(frames.at[r, :], x_s.at[r, cols(h)], own_sem.at[k]).start()
    for i, group in enumerate(local_copies()):
        for src, dst in group:
            pltpu.make_async_copy(src, dst, w_sem.at[i]).start()

    def loaded(i, ref):
        pltpu.make_async_copy(ref, ref, w_sem.at[i]).wait()

    barrier = pltpu.get_barrier_semaphore()

    nx = 4
    nz = nf // nx
    z, x = f // nx, lax.rem(f, nx)

    def frames_peers():
        for dz, dx in farthest_first(nz, nx):
            yield lax.rem(z + dz, nz) * nx + lax.rem(x + dx, nx)

    def greet_h(p, _):
        pl.semaphore_signal(barrier, inc=1, device_id=(f, lax.rem(h + p, nh)), device_id_type=MESH)
        return 0

    for t in frames_peers():
        pl.semaphore_signal(barrier, inc=1, device_id=(t, h), device_id_type=MESH)
    lax.fori_loop(1, nh, greet_h, 0)
    pl.semaphore_wait(barrier, nf + nh - 2)

    L, R, O, S_OWN, S_L, S_R, S_O = range(7)

    def ring(kind, k, src, dst, to):
        return pltpu.make_async_remote_copy(
            src, dst, ring_send, ring_recv.at[kind, k], device_id=(f, to), device_id_type=MESH
        )

    def block(k, who):
        return x_s.at[pl.ds(k * chunk, chunk), cols(who)]

    def arrived(kind, k, who):
        ring(kind, k, block(k, who), block(k, who), sib).wait_recv()

    def pass_on(kind, k, who, to):
        ring(kind, k, block(k, who), block(k, who), to).start()

    evens, odds = range(0, CHUNKS, 2), range(1, CHUNKS, 2)
    for a, b in zip((*evens, *odds), (*odds, *evens)):
        for kind, k, to in ((L, a, right), (R, b, left)):
            ring(kind, k, frames.at[pl.ds(k * chunk, chunk), :], block(k, h), to).start()
    for k in range(CHUNKS):
        ring(S_OWN, k, frames.at[pl.ds(k * chunk, chunk), :], block(k, h), sib).start()

    loaded(0, lat_s)
    loaded(1, cq_s)
    state = lat_s[...].astype(F32)
    q0 = (project(layer_norm(state).astype(BF16), cq_s[0]) * 0.125).astype(BF16)
    qh_s[...] = by_head(q0)
    rows = lat_s[own_rows, :].astype(F32)
    for p in range(passes):
        vt_s[p, pl.ds(LANES, ONES), :] = jnp.ones((ONES, frame_count), BF16)
    loaded(2, ckv_s)

    def normalise(k):
        r = pl.ds(k * chunk, chunk)
        xn_s[r, :] = layer_norm(x_s[r, :].astype(F32)).astype(BF16)

    def keys_values(p, k):
        r = pl.ds(pl.multiple_of(k * chunk, chunk), chunk)
        both = project(xn_s[r, :], ckv_s[:, pl.ds(2 * p * LANES, 2 * LANES)])
        k_s[p, r, :] = both[:, :LANES].astype(BF16)
        vt_s[p, pl.ds(0, LANES), r] = both[:, LANES:].T.astype(BF16)

    def attend(p):
        scores = against(k_s[p], qh_s[...])
        highest = jnp.max(scores, axis=0, keepdims=True)
        m_s[...] = highest
        acc_s[...] = project(vt_s[p], jnp.exp(scores - highest).astype(BF16))

    outstanding = []

    def exchange_f(kind, p, source, there, everything):
        for t in frames_peers():
            pltpu.make_async_remote_copy(
                source(t), there, send_sem.at[p, kind], recv_sem.at[p, kind],
                device_id=(t, h), device_id_type=MESH,
            ).start()
        outstanding.append(lambda: sent(kind, p, everything))

    def landed(kind, p, ref):
        pltpu.make_async_remote_copy(
            ref, ref, send_sem.at[p, kind], recv_sem.at[p, kind], device_id=(f, sib), device_id_type=MESH
        ).wait_recv()

    def sent(kind, p, ref):
        pltpu.make_async_remote_copy(
            ref, ref, send_sem.at[p, kind], recv_sem.at[p, kind], device_id=(f, sib), device_id_type=MESH
        ).wait_send()

    def attend_end(p):
        total = acc_s[pl.ds(LANES, 1), :]
        value = acc_s[pl.ds(0, LANES), :] / total
        both = jnp.concatenate(
            [value[:HEAD_DIM, :latent_count], value[HEAD_DIM:, latent_count:]], axis=0
        )
        o_s[p] = both.T.astype(BF16)
        level = m_s[...] + jnp.log(total)
        for t in range(latent_count // LANES):
            for i in range(2):
                at = i * latent_count + t * LANES
                st_s[p, t, pl.ds(i, 1), :] = level[:, at:at + LANES]

        def rows_of(t):
            return pl.ds(pl.multiple_of(t * rows_each, rows_each), rows_each)

        per_tile = LANES // rows_each
        stats, parts = ps_s.at[p, pl.ds(0, nf - 1)], po_s.at[p, pl.ds(0, nf - 1)]
        exchange_f(STAT, p, lambda t: st_s.at[p, t // per_tile], ps_s.at[p, f], stats)
        exchange_f(PART, p, lambda t: o_s.at[p, rows_of(t), :], po_s.at[p, f], parts)
        po_s[p, f] = o_s[p, own_rows, :]
        ps_s[p, f] = st_s[p, f // per_tile]
        if p + 1 < passes:
            def later(k, _):
                keys_values(p + 1, k)
                return 0

            lax.fori_loop(0, CHUNKS, later, 0)
        landed(STAT, p, stats)
        levels = jnp.concatenate([ps_s[p, :, 0, :], ps_s[p, :, 1, :]], axis=0)
        tr_s[...] = levels.T
        mine = tr_s[pl.ds(pl.multiple_of(lax.rem(f, per_tile) * rows_each, rows_each), rows_each), :]
        weights = []
        for i in range(2):
            level = mine[:, i * nf:(i + 1) * nf]
            e = jnp.exp(level - jnp.max(level, axis=1, keepdims=True))
            weights.append(e / jnp.sum(e, axis=1, keepdims=True))
        landed(PART, p, parts)
        first = lane((rows_each, LANES)) < HEAD_DIM
        context = jnp.zeros((rows_each, LANES), F32)
        for s in range(nf):
            w = jnp.where(first, weights[0][:, s:s + 1], weights[1][:, s:s + 1])
            context += w * po_s[p, s].astype(F32)
        return context.astype(BF16)

    core = lax.rem(h, 2)

    def half_of(c):
        return pl.ds(pl.multiple_of(c * half, half), half)

    def send_midway():
        source, there = row_s.at[:, cols(h)], mid_s.at[own_rows, :]
        exchange_f(MID, 0, lambda t: source, there, mid_s.at[pl.ds(0, latent_count - rows_each), :])
        mid_s[own_rows, :] = row_s[:, cols(h)]

    midway_copy = pltpu.make_async_copy(mid_s, midway, own_sem.at[0])

    def hand_midway():
        landed(MID, 0, mid_s.at[pl.ds(0, latent_count - rows_each)])
        midway_copy.start()

    def head_total(kind, slot, p, left_side, weight, meanwhile=None):
        sum_s[p, slot, h] = project(left_side, weight[p]).astype(BF16)
        for d in (4, 5, 3, 2, 6, 7, 1):
            pltpu.make_async_remote_copy(
                sum_s.at[p, slot, h], sum_s.at[p, slot, h], send_sem.at[p, kind], recv_sem.at[p, kind],
                device_id=(f, lax.rem(h + d, nh)), device_id_type=MESH,
            ).start()
        outstanding.append(lambda: sent(kind, p, sum_s.at[p, slot, pl.ds(0, nh - 1)]))
        if meanwhile is not None:
            meanwhile()
        landed(kind, p, sum_s.at[p, slot, pl.ds(0, nh - 1)])
        out = sum_s[p, slot, 0].astype(F32)
        for i in range(1, nh):
            out += sum_s[p, slot, i].astype(F32)
        return out

    for k in range(CHUNKS):
        kind, onward, who, to = (L, S_L, left, right) if k % 2 == 0 else (R, S_R, right, left)
        arrived(kind, k, who)
        pass_on(O, k, who, to)
        pass_on(onward, k, who, sib)
    for k in (*odds, *evens):
        kind, onward, who = (R, S_R, right) if k % 2 == 0 else (L, S_L, left)
        arrived(kind, k, who)
        pass_on(onward, k, who, sib)
    for j in range(CHUNKS + 1):
        if j < CHUNKS:
            arrived(O, j, opp)
            pass_on(S_O, j, opp, sib)
        if j > 0:
            k = j - 1
            r = pl.ds(k * chunk, chunk)
            pltpu.make_async_copy(frames.at[r, :], x_s.at[r, cols(h)], own_sem.at[k]).wait()
            for kind in (S_OWN, S_L, S_R, S_O):
                arrived(kind, k, sib)
            normalise(k)
            keys_values(0, k)

    for p in range(passes):
        if p > 0:
            qh_s[...] = by_head(qall_s[p])
        attend(p)
        context = attend_end(p)
        if p == 0:
            loaded(3, co_s)
        rows = rows + head_total(CROSS, 0, p, context, co_s)

        if p == 0:
            loaded(4, sqkv_s)
        self_in = layer_norm(rows).astype(BF16)
        others = pl.ds(0, latent_count - rows_each)
        kv = project(self_in, sqkv_s[p, :, pl.ds(LANES, 2 * LANES)])
        for i, (kind, ref) in enumerate(((KEYS, sk_s), (VALUES, sv_s))):
            ref[p, own_rows, :] = kv[:, i * LANES:(i + 1) * LANES].astype(BF16)
            here = ref.at[p, own_rows, :]
            exchange_f(kind, p, lambda t: here, here, ref.at[p, others, :])
        q = by_head((project(self_in, sqkv_s[p, :, pl.ds(0, LANES)]) * 0.125).astype(BF16))
        landed(KEYS, p, sk_s.at[p, others, :])
        scores = against(q, sk_s[p])
        e = jnp.exp(scores - jnp.max(scores, axis=1, keepdims=True))
        weight = (e / jnp.sum(e, axis=1, keepdims=True)).astype(BF16)
        landed(VALUES, p, sv_s.at[p, others, :])
        both = project(weight, sv_s[p])
        first = lane((rows_each, LANES)) < HEAD_DIM
        context = jnp.where(first, both[:rows_each], both[rows_each:]).astype(BF16)
        if p == 0:
            loaded(5, so_s)
        rows = rows + head_total(SELF, 1, p, context, so_s, send_midway if p == 1 else None)

        if p == 0:
            loaded(6, mi_s)
        u = project(layer_norm(rows).astype(BF16), mi_s[p])
        hidden = (0.5 * u * (1.0 + lax.erf(u * 0.7071067811865476))).astype(BF16)
        if p == 0:
            loaded(7, mo_s)
        rows = rows + head_total(MLP, 2, p, hidden, mo_s, hand_midway if p == 1 else None)

        if p + 1 < passes:
            q = (project(layer_norm(rows).astype(BF16), cq_s[p + 1]) * 0.125).astype(BF16)
            qall_s[p + 1, own_rows, :] = q
            here = qall_s.at[p + 1, own_rows, :]
            exchange_f(QUERY, p, lambda t: here, here, qall_s.at[p + 1, others, :])
        if p == 0:
            row_s[...] = rows
        if p + 1 < passes:
            landed(QUERY, p, qall_s.at[p + 1, others, :])

    encoded[...] = rows
    midway_copy.wait()

    ring(0, 0, x_s.at[:, pl.ds(0, 7 * LANES)], x_s.at[:, pl.ds(0, 7 * LANES)], sib).wait_send()
    for wait in outstanding:
        wait()


def hand_over(a, b, a_out, b_out):
    a_out[...] = a[...]
    b_out[...] = b[...]


def local(nf, nh, *args):
    frames, latents, cq, mi = args[0], args[1], args[2], args[10]
    frame_count = frames.shape[0]
    latent_count, width = latents.shape
    passes, hidden = cq.shape[0], mi.shape[2]
    rows_each = latent_count // nf
    vm = pltpu.VMEM
    scratch = [
        vm((frame_count, width), BF16),
        vm((frame_count, width), BF16),
        vm((latent_count, width), BF16),
        vm((passes, width, LANES), BF16),
        vm((width, 2 * passes * LANES), BF16),
        vm((passes, LANES, width), BF16),
        vm((passes, width, 3 * LANES), BF16),
        vm((passes, LANES, width), BF16),
        vm((passes, width, hidden), BF16),
        vm((passes, hidden, width), BF16),
        vm((passes, frame_count, LANES), BF16),
        vm((passes, LANES + ONES, frame_count), BF16),
        vm((passes, latent_count, LANES), BF16),
        vm((2 * latent_count, LANES), BF16),
        vm((1, 2 * latent_count), F32),
        vm((LANES + ONES, 2 * latent_count), F32),
        vm((passes, latent_count, LANES), BF16),
        vm((passes, latent_count // LANES, 2, LANES), F32),
        vm((passes, nf, rows_each, LANES), BF16),
        vm((passes, nf, 2, LANES), F32),
        vm((LANES, 2 * nf), F32),
        vm((passes, latent_count, LANES), BF16),
        vm((passes, latent_count, LANES), BF16),
        vm((passes, 3, rows_each, width // 2), BF16),
        vm((passes, 3, rows_each, width // 2), BF16),
        vm((passes, 3, nh, rows_each, width), BF16),
        vm((rows_each, width), F32),
        vm((latent_count, LANES), F32),
        pltpu.SemaphoreType.DMA((8,)),
        pltpu.SemaphoreType.DMA((CHUNKS,)),
        pltpu.SemaphoreType.DMA((7, CHUNKS)),
        pltpu.SemaphoreType.DMA(()),
        pltpu.SemaphoreType.DMA((passes, 12)),
        pltpu.SemaphoreType.DMA((passes, 12)),
    ]
    outs = pl.pallas_call(
        functools.partial(kernel, nf, nh),
        out_shape=(
            jax.ShapeDtypeStruct((rows_each, width), F32),
            jax.ShapeDtypeStruct((latent_count, LANES), F32),
        ),
        in_specs=[pl.BlockSpec(memory_space=pl.ANY)] * len(args),
        out_specs=(pl.BlockSpec(memory_space=vm), pl.BlockSpec(memory_space=pl.ANY)),
        scratch_shapes=scratch,
        compiler_params=pltpu.CompilerParams(
            collective_id=0, has_side_effects=True, vmem_limit_bytes=56 * 1024 * 1024
        ),
    )(*args)
    return pl.pallas_call(
        hand_over,
        out_shape=tuple(jax.ShapeDtypeStruct(a.shape, a.dtype) for a in outs),
        in_specs=[pl.BlockSpec(memory_space=vm)] * 2,
        out_specs=[pl.BlockSpec(memory_space=vm)] * 2,
    )(*outs)


def solution(mesh):
    nf, nh = mesh.shape["frames"], mesh.shape["heads"]
    by_column, by_row = P(None, None, "heads"), P(None, "heads", None)
    placed = (
        P("frames", "heads"), P(),
        by_column, by_column, by_column, by_row,
        by_column, by_column, by_column, by_row,
        by_column, by_row,
    )
    return jax.shard_map(
        functools.partial(local, nf, nh),
        mesh=mesh,
        in_specs=placed,
        out_specs=(P("frames", None), P(None, "heads")),
        check_vma=False,
    )
```

```python
import functools

import jax
import jax.numpy as jnp
from jax import lax
from jax.experimental import pallas as pl
from jax.experimental.pallas import tpu as pltpu
from jax.sharding import PartitionSpec as P

EPSILON = 1e-05
HEAD_DIM = 64
MESH = pl.DeviceIdType.MESH
F32 = jnp.float32
BF16 = jnp.bfloat16
CHUNKS = 4
LANES = 128
ONES = 16
PART, STAT, KEYS, VALUES, QUERY, MID, CROSS, SELF, MLP = range(9)
PAIRS = 3


def layer_norm(v):
    centre = v - jnp.mean(v, axis=-1, keepdims=True)
    spread = jnp.mean(centre * centre, axis=-1, keepdims=True)
    return centre * lax.rsqrt(spread + EPSILON)


def project(a, b):
    return jnp.dot(a, b, preferred_element_type=F32)


def against(a, b):
    return lax.dot_general(a, b, (((1,), (1,)), ((), ())), preferred_element_type=F32)


def lane(shape):
    return lax.broadcasted_iota(jnp.int32, shape, len(shape) - 1)


def by_head(q):
    first = lane(q.shape) < HEAD_DIM
    zero = jnp.zeros_like(q)
    return jnp.concatenate([jnp.where(first, q, zero), jnp.where(first, zero, q)], axis=0)


def farthest_first(nz, nx):
    steps = [(dz, dx) for dz in range(nz) for dx in range(nx) if dz or dx]
    return sorted(steps, key=lambda s: -(min(s[0], nz - s[0]) + min(s[1], nx - s[1])))


def kernel(
    nf, nh,
    frames, latents, cq, ck, cv, co, sq, sk, sv, so, mi, mo,
    encoded, midway,
    x_s, xn_s, lat_s, cq_s, ckv_s, co_s, sqkv_s, so_s, mi_s, mo_s,
    k_s, vt_s, qall_s, qh_s, m_s, acc_s, o_s, st_s, po_s, ps_s, tr_s, sk_s, sv_s, give_s, take_s, sum_s, row_s, mid_s,
    w_sem, own_sem, ring_recv, ring_send, recv_sem, send_sem,
):
    f, h = lax.axis_index("frames"), lax.axis_index("heads")
    latent_count, width = lat_s.shape
    frame_count = x_s.shape[0]
    rows_each = latent_count // nf
    chunk = frame_count // CHUNKS
    half = width // 2
    passes = cq_s.shape[0]

    sib = h + 1 - 2 * lax.rem(h, 2)
    right, left, opp = lax.rem(h + 2, nh), lax.rem(h + nh - 2, nh), lax.rem(h + 4, nh)

    def cols(who):
        return pl.ds(pl.multiple_of(who * LANES, LANES), LANES)

    own_rows = pl.ds(pl.multiple_of(f * rows_each, rows_each), rows_each)

    def local_copies():
        groups = [
            [(latents, lat_s)],
            [(cq, cq_s)],
            [(w.at[p], ckv_s.at[:, pl.ds((2 * p + i) * LANES, LANES)]) for p in range(passes) for i, w in enumerate((ck, cv))],
            [(co, co_s)],
            [(w, sqkv_s.at[:, :, pl.ds(i * LANES, LANES)]) for i, w in enumerate((sq, sk, sv))],
            [(so, so_s)],
            [(mi, mi_s)],
            [(mo, mo_s)],
        ]
        return groups

    for k in range(CHUNKS):
        r = pl.ds(k * chunk, chunk)
        pltpu.make_async_copy(frames.at[r, :], x_s.at[r, cols(h)], own_sem.at[k]).start()
    for i, group in enumerate(local_copies()):
        for src, dst in group:
            pltpu.make_async_copy(src, dst, w_sem.at[i]).start()

    def loaded(i, ref):
        pltpu.make_async_copy(ref, ref, w_sem.at[i]).wait()

    barrier = pltpu.get_barrier_semaphore()

    nx = 4
    nz = nf // nx
    z, x = f // nx, lax.rem(f, nx)

    def frames_peers():
        for dz, dx in farthest_first(nz, nx):
            yield lax.rem(z + dz, nz) * nx + lax.rem(x + dx, nx)

    def greet_h(p, _):
        pl.semaphore_signal(barrier, inc=1, device_id=(f, lax.rem(h + p, nh)), device_id_type=MESH)
        return 0

    for t in frames_peers():
        pl.semaphore_signal(barrier, inc=1, device_id=(t, h), device_id_type=MESH)
    lax.fori_loop(1, nh, greet_h, 0)
    pl.semaphore_wait(barrier, nf + nh - 2)

    L, R, O, S_OWN, S_L, S_R, S_O = range(7)

    def ring(kind, k, src, dst, to):
        return pltpu.make_async_remote_copy(
            src, dst, ring_send, ring_recv.at[kind, k], device_id=(f, to), device_id_type=MESH
        )

    def block(k, who):
        return x_s.at[pl.ds(k * chunk, chunk), cols(who)]

    def arrived(kind, k, who):
        ring(kind, k, block(k, who), block(k, who), sib).wait_recv()

    def pass_on(kind, k, who, to):
        ring(kind, k, block(k, who), block(k, who), to).start()

    evens, odds = range(0, CHUNKS, 2), range(1, CHUNKS, 2)
    for a, b in zip((*evens, *odds), (*odds, *evens)):
        for kind, k, to in ((L, a, right), (R, b, left)):
            ring(kind, k, frames.at[pl.ds(k * chunk, chunk), :], block(k, h), to).start()
    for k in range(CHUNKS):
        ring(S_OWN, k, frames.at[pl.ds(k * chunk, chunk), :], block(k, h), sib).start()

    loaded(0, lat_s)
    loaded(1, cq_s)
    state = lat_s[...].astype(F32)
    q0 = (project(layer_norm(state).astype(BF16), cq_s[0]) * 0.125).astype(BF16)
    qh_s[...] = by_head(q0)
    rows = lat_s[own_rows, :].astype(F32)
    for p in range(passes):
        vt_s[p, pl.ds(LANES, ONES), :] = jnp.ones((ONES, frame_count), BF16)
    loaded(2, ckv_s)

    def normalise(k):
        r = pl.ds(k * chunk, chunk)
        xn_s[r, :] = layer_norm(x_s[r, :].astype(F32)).astype(BF16)

    def keys_values(p, k):
        r = pl.ds(pl.multiple_of(k * chunk, chunk), chunk)
        both = project(xn_s[r, :], ckv_s[:, pl.ds(2 * p * LANES, 2 * LANES)])
        k_s[p, r, :] = both[:, :LANES].astype(BF16)
        vt_s[p, pl.ds(0, LANES), r] = both[:, LANES:].T.astype(BF16)

    def attend(p):
        scores = against(k_s[p], qh_s[...])
        highest = jnp.max(scores, axis=0, keepdims=True)
        m_s[...] = highest
        acc_s[...] = project(vt_s[p], jnp.exp(scores - highest).astype(BF16))

    outstanding = []

    def exchange_f(kind, p, source, there, everything):
        for t in frames_peers():
            pltpu.make_async_remote_copy(
                source(t), there, send_sem.at[p, kind], recv_sem.at[p, kind],
                device_id=(t, h), device_id_type=MESH,
            ).start()
        outstanding.append(lambda: sent(kind, p, everything))

    def landed(kind, p, ref):
        pltpu.make_async_remote_copy(
            ref, ref, send_sem.at[p, kind], recv_sem.at[p, kind], device_id=(f, sib), device_id_type=MESH
        ).wait_recv()

    def sent(kind, p, ref):
        pltpu.make_async_remote_copy(
            ref, ref, send_sem.at[p, kind], recv_sem.at[p, kind], device_id=(f, sib), device_id_type=MESH
        ).wait_send()

    def attend_end(p):
        total = acc_s[pl.ds(LANES, 1), :]
        level = m_s[...] + jnp.log(total)
        for t in range(latent_count // LANES):
            for i in range(2):
                at = i * latent_count + t * LANES
                st_s[p, t, pl.ds(i, 1), :] = level[:, at:at + LANES]

        def rows_of(t):
            return pl.ds(pl.multiple_of(t * rows_each, rows_each), rows_each)

        per_tile = LANES // rows_each
        stats, parts = ps_s.at[p, pl.ds(0, nf - 1)], po_s.at[p, pl.ds(0, nf - 1)]
        exchange_f(STAT, p, lambda t: st_s.at[p, t // per_tile], ps_s.at[p, f], stats)
        value = acc_s[pl.ds(0, LANES), :] / total
        both = jnp.concatenate(
            [value[:HEAD_DIM, :latent_count], value[HEAD_DIM:, latent_count:]], axis=0
        )
        o_s[p] = both.T.astype(BF16)
        exchange_f(PART, p, lambda t: o_s.at[p, rows_of(t), :], po_s.at[p, f], parts)
        po_s[p, f] = o_s[p, own_rows, :]
        ps_s[p, f] = st_s[p, f // per_tile]
        if p + 1 < passes:
            def later(k, _):
                keys_values(p + 1, k)
                return 0

            lax.fori_loop(0, CHUNKS, later, 0)
        landed(STAT, p, stats)
        levels = jnp.concatenate([ps_s[p, :, 0, :], ps_s[p, :, 1, :]], axis=0)
        tr_s[...] = levels.T
        mine = tr_s[pl.ds(pl.multiple_of(lax.rem(f, per_tile) * rows_each, rows_each), rows_each), :]
        weights = []
        for i in range(2):
            level = mine[:, i * nf:(i + 1) * nf]
            e = jnp.exp(level - jnp.max(level, axis=1, keepdims=True))
            weights.append(e / jnp.sum(e, axis=1, keepdims=True))
        landed(PART, p, parts)
        first = lane((rows_each, LANES)) < HEAD_DIM
        context = jnp.zeros((rows_each, LANES), F32)
        for s in range(nf):
            w = jnp.where(first, weights[0][:, s:s + 1], weights[1][:, s:s + 1])
            context += w * po_s[p, s].astype(F32)
        return context.astype(BF16)

    core = lax.rem(h, 2)

    def half_of(c):
        return pl.ds(pl.multiple_of(c * half, half), half)

    def send_midway():
        source, there = row_s.at[:, cols(h)], mid_s.at[own_rows, :]
        exchange_f(MID, 0, lambda t: source, there, mid_s.at[pl.ds(0, latent_count - rows_each), :])
        mid_s[own_rows, :] = row_s[:, cols(h)]

    midway_copy = pltpu.make_async_copy(mid_s, midway, own_sem.at[0])

    def hand_midway():
        landed(MID, 0, mid_s.at[pl.ds(0, latent_count - rows_each)])
        midway_copy.start()

    def head_total(kind, slot, p, left_side, weight, meanwhile=None):
        sum_s[p, slot, h] = project(left_side, weight[p]).astype(BF16)
        for d in (4, 5, 3, 2, 6, 7, 1):
            pltpu.make_async_remote_copy(
                sum_s.at[p, slot, h], sum_s.at[p, slot, h], send_sem.at[p, kind], recv_sem.at[p, kind],
                device_id=(f, lax.rem(h + d, nh)), device_id_type=MESH,
            ).start()
        outstanding.append(lambda: sent(kind, p, sum_s.at[p, slot, pl.ds(0, nh - 1)]))
        if meanwhile is not None:
            meanwhile()
        landed(kind, p, sum_s.at[p, slot, pl.ds(0, nh - 1)])
        out = sum_s[p, slot, 0].astype(F32)
        for i in range(1, nh):
            out += sum_s[p, slot, i].astype(F32)
        return out

    for k in range(CHUNKS):
        kind, onward, who, to = (L, S_L, left, right) if k % 2 == 0 else (R, S_R, right, left)
        arrived(kind, k, who)
        pass_on(O, k, who, to)
        pass_on(onward, k, who, sib)
    for k in (*odds, *evens):
        kind, onward, who = (R, S_R, right) if k % 2 == 0 else (L, S_L, left)
        arrived(kind, k, who)
        pass_on(onward, k, who, sib)
    for j in range(CHUNKS + 1):
        if j < CHUNKS:
            arrived(O, j, opp)
            pass_on(S_O, j, opp, sib)
        if j > 0:
            k = j - 1
            r = pl.ds(k * chunk, chunk)
            pltpu.make_async_copy(frames.at[r, :], x_s.at[r, cols(h)], own_sem.at[k]).wait()
            for kind in (S_OWN, S_L, S_R, S_O):
                arrived(kind, k, sib)
            normalise(k)
            keys_values(0, k)

    for p in range(passes):
        if p > 0:
            qh_s[...] = by_head(qall_s[p])
        attend(p)
        context = attend_end(p)
        if p == 0:
            loaded(3, co_s)
        rows = rows + head_total(CROSS, 0, p, context, co_s)

        if p == 0:
            loaded(4, sqkv_s)
        self_in = layer_norm(rows).astype(BF16)
        others = pl.ds(0, latent_count - rows_each)
        kv = project(self_in, sqkv_s[p, :, pl.ds(LANES, 2 * LANES)])
        for i, (kind, ref) in enumerate(((KEYS, sk_s), (VALUES, sv_s))):
            ref[p, own_rows, :] = kv[:, i * LANES:(i + 1) * LANES].astype(BF16)
            here = ref.at[p, own_rows, :]
            exchange_f(kind, p, lambda t: here, here, ref.at[p, others, :])
        q = by_head((project(self_in, sqkv_s[p, :, pl.ds(0, LANES)]) * 0.125).astype(BF16))
        landed(KEYS, p, sk_s.at[p, others, :])
        scores = against(q, sk_s[p])
        e = jnp.exp(scores - jnp.max(scores, axis=1, keepdims=True))
        weight = (e / jnp.sum(e, axis=1, keepdims=True)).astype(BF16)
        landed(VALUES, p, sv_s.at[p, others, :])
        both = project(weight, sv_s[p])
        first = lane((rows_each, LANES)) < HEAD_DIM
        context = jnp.where(first, both[:rows_each], both[rows_each:]).astype(BF16)
        if p == 0:
            loaded(5, so_s)
        rows = rows + head_total(SELF, 1, p, context, so_s, send_midway if p == 1 else None)

        if p == 0:
            loaded(6, mi_s)
        u = project(layer_norm(rows).astype(BF16), mi_s[p])
        hidden = (0.5 * u * (1.0 + lax.erf(u * 0.7071067811865476))).astype(BF16)
        if p == 0:
            loaded(7, mo_s)
        rows = rows + head_total(MLP, 2, p, hidden, mo_s, hand_midway if p == 1 else None)

        if p + 1 < passes:
            q = (project(layer_norm(rows).astype(BF16), cq_s[p + 1]) * 0.125).astype(BF16)
            qall_s[p + 1, own_rows, :] = q
            here = qall_s.at[p + 1, own_rows, :]
            exchange_f(QUERY, p, lambda t: here, here, qall_s.at[p + 1, others, :])
        if p == 0:
            row_s[...] = rows
        if p + 1 < passes:
            landed(QUERY, p, qall_s.at[p + 1, others, :])

    encoded[...] = rows
    midway_copy.wait()

    ring(0, 0, x_s.at[:, pl.ds(0, 7 * LANES)], x_s.at[:, pl.ds(0, 7 * LANES)], sib).wait_send()
    for wait in outstanding:
        wait()


def hand_over(a, b, a_out, b_out):
    a_out[...] = a[...]
    b_out[...] = b[...]


def local(nf, nh, *args):
    frames, latents, cq, mi = args[0], args[1], args[2], args[10]
    frame_count = frames.shape[0]
    latent_count, width = latents.shape
    passes, hidden = cq.shape[0], mi.shape[2]
    rows_each = latent_count // nf
    vm = pltpu.VMEM
    scratch = [
        vm((frame_count, width), BF16),
        vm((frame_count, width), BF16),
        vm((latent_count, width), BF16),
        vm((passes, width, LANES), BF16),
        vm((width, 2 * passes * LANES), BF16),
        vm((passes, LANES, width), BF16),
        vm((passes, width, 3 * LANES), BF16),
        vm((passes, LANES, width), BF16),
        vm((passes, width, hidden), BF16),
        vm((passes, hidden, width), BF16),
        vm((passes, frame_count, LANES), BF16),
        vm((passes, LANES + ONES, frame_count), BF16),
        vm((passes, latent_count, LANES), BF16),
        vm((2 * latent_count, LANES), BF16),
        vm((1, 2 * latent_count), F32),
        vm((LANES + ONES, 2 * latent_count), F32),
        vm((passes, latent_count, LANES), BF16),
        vm((passes, latent_count // LANES, 2, LANES), F32),
        vm((passes, nf, rows_each, LANES), BF16),
        vm((passes, nf, 2, LANES), F32),
        vm((LANES, 2 * nf), F32),
        vm((passes, latent_count, LANES), BF16),
        vm((passes, latent_count, LANES), BF16),
        vm((passes, 3, rows_each, width // 2), BF16),
        vm((passes, 3, rows_each, width // 2), BF16),
        vm((passes, 3, nh, rows_each, width), BF16),
        vm((rows_each, width), F32),
        vm((latent_count, LANES), F32),
        pltpu.SemaphoreType.DMA((8,)),
        pltpu.SemaphoreType.DMA((CHUNKS,)),
        pltpu.SemaphoreType.DMA((7, CHUNKS)),
        pltpu.SemaphoreType.DMA(()),
        pltpu.SemaphoreType.DMA((passes, 12)),
        pltpu.SemaphoreType.DMA((passes, 12)),
    ]
    outs = pl.pallas_call(
        functools.partial(kernel, nf, nh),
        out_shape=(
            jax.ShapeDtypeStruct((rows_each, width), F32),
            jax.ShapeDtypeStruct((latent_count, LANES), F32),
        ),
        in_specs=[pl.BlockSpec(memory_space=pl.ANY)] * len(args),
        out_specs=(pl.BlockSpec(memory_space=vm), pl.BlockSpec(memory_space=pl.ANY)),
        scratch_shapes=scratch,
        compiler_params=pltpu.CompilerParams(
            collective_id=0, has_side_effects=True, vmem_limit_bytes=56 * 1024 * 1024
        ),
    )(*args)
    return pl.pallas_call(
        hand_over,
        out_shape=tuple(jax.ShapeDtypeStruct(a.shape, a.dtype) for a in outs),
        in_specs=[pl.BlockSpec(memory_space=vm)] * 2,
        out_specs=[pl.BlockSpec(memory_space=vm)] * 2,
    )(*outs)


def solution(mesh):
    nf, nh = mesh.shape["frames"], mesh.shape["heads"]
    by_column, by_row = P(None, None, "heads"), P(None, "heads", None)
    placed = (
        P("frames", "heads"), P(),
        by_column, by_column, by_column, by_row,
        by_column, by_column, by_column, by_row,
        by_column, by_row,
    )
    return jax.shard_map(
        functools.partial(local, nf, nh),
        mesh=mesh,
        in_specs=placed,
        out_specs=(P("frames", None), P(None, "heads")),
        check_vma=False,
    )
```
